256 devices in a mesh: section: 16 (over y, x), dp: 16 (over z, core).
Axes of the slice: x: 4, y: 4, z: 8, core: 2. Of those that a mesh axis runs over, the one named last changes fastest.
Arguments:
- inputs: bfloat16 [8, 256, 2560], P(None, 'dp'), may hold values from -6 to 6
- cotangent: bfloat16 [8, 256, 2560], P(None, 'dp'), may hold values from -6 to 6
- weights: bfloat16 [16, 2560, 2560], P('section', 'dp'), may hold values from -0.0625 to 0.0625
- old_factor: float32 [16, 8, 640, 640], P('section', None, 'dp'), as said below
- plan: int32 [16, 3], replicated, may hold values from 0 to 15, as said below
- order: int32 [8], replicated, may hold values from 0 to 7, each once
Outputs:
- section_out: bfloat16 [16, 8, 256, 2560], P('section', None, 'dp')
- section_grad: bfloat16 [16, 8, 256, 2560], P('section', None, 'dp')
- inverse: float32 [16, 640, 640], P('section', 'dp')
The draws below stay inside these ranges and needn't reach their ends.
Inputs may be any that keep to these rules, and one draw needn't show every extreme that they name: plan[s, 0] is a block of 0 to 7; plan[s, 1] is s or (s + 8) mod 16; plan[s, 2] is 1 to 8. `old_factor`: each block is symmetric with a positive diagonal that exceeds the sum of the absolute values of the rest of its row.
All inputs are finite; a program needn't handle non-finite values. Where the reference program divides by a largest or mean magnitude, that divisor is 1e-20 or more.
Results may differ from the reference program's by a relative error of at most 0.023.
Values may be sent and summed in bfloat16 or wider, within the bound.
A program may use at most 64 MiB of HBM per device.

```python
import math
import jax
import jax.numpy as jnp
from jax import lax

D = 2560
B = 640
MICRO = 8
ITERS = 3
NB = 8
TOK = 256
N_SECTION = 16


def draw_plan(key, part):
    key = jax.random.fold_in(key, 11)
    key_blocks, key_moves, key_slots = jax.random.split(key, 3)
    section_ids = jnp.arange(N_SECTION, dtype=jnp.int32)
    block_ids = jax.random.randint(key_blocks, (N_SECTION,), 0, NB, dtype=jnp.int32)
    block_ids = block_ids.at[0].set(NB - 1).at[N_SECTION - 1].set(0)
    moved_flag = jax.random.randint(key_moves, (N_SECTION,), 0, 2, dtype=jnp.int32)
    moved_flag = moved_flag.at[0].set(1).at[N_SECTION // 2 - 1].set(1).at[N_SECTION // 2].set(1).at[N_SECTION - 1].set(1)
    executors = (section_ids + moved_flag * (N_SECTION // 2)) % N_SECTION
    slot_values = jax.random.randint(key_slots, (N_SECTION,), 1, MICRO + 1, dtype=jnp.int32)
    slot_values = slot_values.at[0].set(MICRO).at[N_SECTION - 1].set(1)
    return jnp.stack([block_ids, executors, slot_values], axis=1).astype(jnp.int32)


def draw_old_factor(key, part):
    key = jax.random.fold_in(key, 23)
    key_diag, key_noise = jax.random.split(key)
    diagonal = jnp.exp(jax.random.uniform(key_diag, (N_SECTION, NB, B), jnp.float32, 0.0, math.log(10.0)))
    noise_vals = jax.random.uniform(key_noise, (N_SECTION, NB, B, B), jnp.float32, -1.0, 1.0)
    symmetric = 0.5 * (noise_vals + jnp.swapaxes(noise_vals, 2, 3))
    smaller = jnp.minimum(diagonal[:, :, :, None], diagonal[:, :, None, :])
    identity = jnp.eye(B, dtype=jnp.float32)
    off_part = symmetric * smaller * (0.9 / B) * (1.0 - identity)
    return (off_part + identity * diagonal[:, :, :, None]).astype(jnp.float32)


def level_of(key, shape, cuts, smallest, top_value):
    level = 1.0
    for dim, parts in cuts:
        steps = jax.random.uniform(jax.random.fold_in(jax.random.fold_in(key, 6), dim), (parts,), jnp.float32, smallest / len(cuts), top_value / len(cuts))
        level = level * jnp.repeat(jnp.exp(steps), shape[dim] // parts).reshape((-1,) + (1,) * (len(shape) - 1 - dim))
    return level


def gaussian(own_key, shape, deviation, bound, pieces=(), held_as=jnp.bfloat16):
    array = deviation * jax.random.normal(own_key, shape, jnp.float32)
    if pieces:
        array = array * level_of(own_key, shape, pieces, -0.22, 0.18)
    return jnp.clip(array, -bound, bound).astype(held_as)


def setup_inputs(seed: int = 0) -> dict:
    arg_keys = jax.random.split(jax.random.key(seed), 7)
    return {
        "inputs": gaussian(arg_keys[0], (MICRO, TOK, D), 1.0, 6.0, ((1, 16),)),
        "cotangent": gaussian(arg_keys[1], (MICRO, TOK, D), 1.0, 6.0, ((1, 16),)),
        "weights": gaussian(arg_keys[2], (N_SECTION, D, D), (4 * D) ** -0.5, 0.0625, ((0, 16), (1, 16))),
        "old_factor": draw_old_factor(jax.random.fold_in(arg_keys[6], 71), 0),
        "plan": draw_plan(jax.random.fold_in(arg_keys[6], 71), 0),
        "order": jax.random.permutation(arg_keys[5], MICRO).astype(jnp.int32),
    }


RETAIN = 0.6
DAMPING = 0.1


def newton_schulz(matrix):
    order_size = matrix.shape[0]
    identity = jnp.eye(order_size, dtype=jnp.float32)
    row_bound = jnp.max(jnp.sum(jnp.abs(matrix), axis=1))
    approx = identity / row_bound
    for iteration in range(ITERS):
        product = jnp.dot(matrix, approx, precision=lax.Precision.HIGHEST, preferred_element_type=jnp.float32)
        approx = jnp.dot(approx, 2.0 * identity - product, precision=lax.Precision.HIGHEST, preferred_element_type=jnp.float32)
    return approx


def reference(inputs, cotangent, weights, old_factor, plan, order):
    half_count = NB // 2
    current = jnp.take(inputs, order, axis=0).reshape(MICRO * TOK, D)
    section_inputs = []
    section_pre = []
    outputs = []
    for section_id in range(N_SECTION):
        preact = jnp.dot(current, weights[section_id], preferred_element_type=jnp.float32)
        output = (current.astype(jnp.float32) + jax.nn.silu(preact)).astype(jnp.bfloat16)
        section_inputs.append(current)
        section_pre.append(preact)
        outputs.append(output)
        current = output
    upstream = jnp.take(cotangent, order, axis=0).reshape(MICRO * TOK, D)
    gradients = [None] * N_SECTION
    deltas = [None] * N_SECTION
    for section_id in reversed(range(N_SECTION)):
        preact = section_pre[section_id]
        gating = jax.nn.sigmoid(preact)
        delta_now = (upstream.astype(jnp.float32) * gating * (1.0 + preact * (1.0 - gating))).astype(jnp.bfloat16)
        backward = lax.dot_general(delta_now, weights[section_id], (((1,), (1,)), ((), ())), preferred_element_type=jnp.float32)
        upstream = (upstream.astype(jnp.float32) + backward).astype(jnp.bfloat16)
        gradients[section_id] = upstream
        deltas[section_id] = delta_now
    positions = (jnp.arange(MICRO * TOK) // TOK).astype(jnp.int32)
    identity = jnp.eye(B, dtype=jnp.float32)
    inverses = []
    for section_id in range(N_SECTION):
        block_id = plan[section_id, 0].astype(jnp.int32)
        filled = plan[section_id, 2].astype(jnp.int32)
        offset = ((block_id % half_count) * B).astype(jnp.int32)
        from_inputs = lax.dynamic_slice_in_dim(section_inputs[section_id], offset, B, 1)
        from_deltas = lax.dynamic_slice_in_dim(deltas[section_id], offset, B, 1)
        features = jnp.where(block_id < half_count, from_inputs, from_deltas)
        masked = jnp.where((positions < filled)[:, None], features, jnp.zeros_like(features))
        fresh_sum = lax.dot_general(masked, features, (((0,), (0,)), ((), ())), preferred_element_type=jnp.float32)
        fresh_mean = fresh_sum / (filled * TOK).astype(jnp.float32)
        old_block = lax.dynamic_index_in_dim(old_factor[section_id], block_id, 0, keepdims=False)
        matrix = RETAIN * old_block + (1.0 - RETAIN) * fresh_mean + DAMPING * identity
        inverses.append(newton_schulz(matrix))
    section_out = jnp.stack(outputs).reshape(N_SECTION, MICRO, TOK, D)
    section_grad = jnp.stack(gradients).reshape(N_SECTION, MICRO, TOK, D)
    return (section_out, section_grad, jnp.stack(inverses))
```

```python
import functools

import jax
import jax.numpy as jnp
from jax import lax
from jax.experimental import pallas as pl
from jax.experimental.pallas import tpu as pltpu
from jax.sharding import PartitionSpec as P

RETAIN = 0.6
DAMPING = 0.1
TERMS = 8
CORES = 2
MESH = pl.DeviceIdType.MESH


def kernel(
    sections,
    replicas,
    pieces,
    plan_ref,
    order_ref,
    x_ref,
    ct_ref,
    w_ref,
    old_ref,
    out_ref,
    grad_ref,
    inv_ref,
    w,
    wt,
    x_in,
    g_in,
    slope,
    delta,
    feats,
    old_all,
    matrix,
    local_sem,
    ring_send,
    ring_recv,
    sib_sem,
    fwd_send,
    fwd_recv,
    bwd_send,
    bwd_recv,
    feat_send,
    feat_recv,
    old_sem,
):
    micro, rows, width = x_in.shape
    shard = w_ref.shape[1]
    half = shard // 2
    band, order_size = old_ref.shape[2], old_ref.shape[3]
    piece = width // pieces
    zs = replicas // CORES
    s = lax.axis_index("section")
    r = lax.axis_index("dp")
    z, core = r // CORES, r % CORES
    first, last = s == 0, s == sections - 1
    z_right, z_left = (z + 1) % zs, (z + zs - 1) % zs
    right, left = z_right * CORES + core, z_left * CORES + core
    sibling = z * CORES + (1 - core)
    up, down = jnp.minimum(s + 1, sections - 1), jnp.maximum(s - 1, 0)

    barrier = pltpu.get_barrier_semaphore()

    def greet(i, _):
        pl.semaphore_signal(
            barrier, inc=1, device_id={"dp": (r + i) % replicas}, device_id_type=MESH
        )
        return 0

    lax.fori_loop(1, replicas, greet, 0)

    @pl.when(jnp.logical_not(last))
    def _():
        pl.semaphore_signal(barrier, inc=1, device_id={"section": up}, device_id_type=MESH)

    @pl.when(jnp.logical_not(first))
    def _():
        pl.semaphore_signal(barrier, inc=1, device_id={"section": down}, device_id_type=MESH)

    peers = replicas - 1 + jnp.where(first, 0, 1) + jnp.where(last, 0, 1)
    pl.semaphore_wait(barrier, peers)

    def w_rows(at_z, which):
        start = (at_z * CORES + core) * shard + which * half
        return w.at[pl.ds(pl.multiple_of(start, 16), half)]

    def copy(src, dst, send, recv, **device):
        return pltpu.make_async_remote_copy(
            src_ref=src,
            dst_ref=dst,
            send_sem=send,
            recv_sem=recv,
            device_id=device,
            device_id_type=MESH,
        )

    own_w = pltpu.make_async_copy(
        w_ref.at[0], w.at[pl.ds(pl.multiple_of(r * shard, 16), shard)], local_sem
    )

    def to_sibling(at_z, which):
        rows_there = w_rows(at_z, which)
        copy(rows_there, rows_there, sib_sem.at[0], sib_sem.at[1], dp=sibling).start()

    def ring_send_of(way, k):
        hop, which = k // 2, (k + way) % 2
        dst = w_rows((z + zs - hop) % zs if way == 0 else (z + hop) % zs, which)
        src = w_ref.at[0, pl.ds(which * half, half)] if hop == 0 else dst
        there = right if way == 0 else left
        return copy(src, dst, ring_send.at[way, k], ring_recv.at[way, k], dp=there)

    def ring_arrival(way, k):
        hop, which = k // 2 + 1, (k + way) % 2
        at_z = (z + zs - hop) % zs if way == 0 else (z + hop) % zs
        here = w_rows(at_z, which)
        there = right if way == 0 else left
        copy(here, here, ring_send.at[way, k], ring_recv.at[way, k], dp=there).wait_recv()
        return at_z, which

    own_w.start()
    for k in range(zs - 1):
        for way in range(2):
            came = ring_arrival(way, k - 2) if k >= 2 else None
            ring_send_of(way, k).start()
            if came:
                to_sibling(*came)
        if k == 0:
            own_w.wait()
        if k == 1:
            to_sibling(z, 0)
            to_sibling(z, 1)
    for k in range(zs - 3, zs - 1):
        for way in range(2):
            to_sibling(*ring_arrival(way, k))
    for k in range(zs - 1):
        for way in range(2):
            ring_send_of(way, k).wait_send()
    all_sib = w.at[pl.ds(0, zs * shard)]
    sib_wait = copy(all_sib, all_sib, sib_sem.at[0], sib_sem.at[1], dp=sibling)
    sib_wait.wait_recv()
    sib_wait.wait_send()

    block = plan_ref[s, 0]
    filled = plan_ref[s, 2]
    old_all[r] = old_ref[0, block]

    def send_old(i, _):
        copy(
            old_all.at[r], old_all.at[r], old_sem.at[0], old_sem.at[1], dp=(r + i) % replicas
        ).start()
        return 0

    lax.fori_loop(1, replicas, send_old, 0)

    def turn_weights():
        tile = 2 * 128
        spots = lax.broadcasted_iota(jnp.int32, (tile, tile), 0)
        eye = (spots == lax.broadcasted_iota(jnp.int32, (tile, tile), 1)).astype(jnp.bfloat16)

        def turn(i, _):
            at = pl.ds(pl.multiple_of(i * tile, tile), tile)
            for j in range(pieces):
                cols = pl.ds(j * piece, piece)
                wt[cols, at] = lax.dot_general(
                    w[at, cols], eye, (((0,), (0,)), ((), ())), preferred_element_type=jnp.float32
                ).astype(jnp.bfloat16)
            return 0

        lax.fori_loop(0, width // tile, turn, 0)

    @pl.when(s >= sections // 2)
    def _():
        turn_weights()

    def forward(c, _):
        @pl.when(first)
        def _():
            x_in[c] = x_ref[order_ref[c]]

        @pl.when(jnp.logical_not(first))
        def _():
            copy(x_in.at[c], x_in.at[c], fwd_send.at[c], fwd_recv.at[c], section=up).wait_recv()

        x = x_in[c]
        for j in range(pieces):
            cols = pl.ds(j * piece, piece)
            pre = jnp.dot(x, w[:, cols], preferred_element_type=jnp.float32)
            gate = jax.nn.sigmoid(pre)
            out_ref[0, c, :, cols] = (
                x_in[c, :, cols].astype(jnp.float32) + pre * gate
            ).astype(jnp.bfloat16)

            @pl.when(jnp.logical_not(last))
            def _():
                copy(
                    out_ref.at[0, c, :, cols],
                    x_in.at[c, :, cols],
                    fwd_send.at[c],
                    fwd_recv.at[c],
                    section=up,
                ).start()

            slope[c, :, cols] = gate * (1.0 + pre * (1.0 - gate))
        return 0

    lax.fori_loop(0, micro, forward, 0)

    @pl.when(s < sections // 2)
    def _():
        turn_weights()

    place = block % (width // order_size)
    from_input = block < width // order_size

    def backward(c, _):
        @pl.when(last)
        def _():
            g_in[c] = ct_ref[order_ref[c]]

        @pl.when(jnp.logical_not(last))
        def _():
            copy(g_in.at[c], g_in.at[c], bwd_send.at[c], bwd_recv.at[c], section=down).wait_recv()

        delta[...] = (g_in[c].astype(jnp.float32) * slope[c]).astype(jnp.bfloat16)
        d = delta[...]
        for j in range(pieces):
            cols = pl.ds(j * piece, piece)
            back = jnp.dot(d, wt[:, cols], preferred_element_type=jnp.float32)
            grad_ref[0, c, :, cols] = (g_in[c, :, cols].astype(jnp.float32) + back).astype(
                jnp.bfloat16
            )

            @pl.when(jnp.logical_not(first))
            def _():
                copy(
                    grad_ref.at[0, c, :, cols],
                    g_in.at[c, :, cols],
                    bwd_send.at[c],
                    bwd_recv.at[c],
                    section=down,
                ).start()

        chosen = jnp.zeros((rows, order_size), jnp.bfloat16)
        for j in range(width // order_size):
            cols = pl.ds(j * order_size, order_size)
            here = jnp.where(from_input, x_in[c, :, cols], delta[:, cols])
            chosen = jnp.where(place == j, here, chosen)
        feats[c, r] = jnp.where(c < filled, chosen, jnp.zeros_like(chosen))

        def send_feats(i, _):
            copy(
                feats.at[c, r],
                feats.at[c, r],
                feat_send.at[c],
                feat_recv.at[c],
                dp=(r + i) % replicas,
            ).start()
            return 0

        lax.fori_loop(1, replicas, send_feats, 0)
        return 0

    lax.fori_loop(0, micro, backward, 0)

    matrix[...] = jnp.zeros_like(matrix)

    def gather_stats(c, _):
        others = feats.at[c, pl.ds(0, replicas - 1)]
        copy(others, others, feat_send.at[c], feat_recv.at[c], dp=sibling).wait_recv()
        v = feats[c].reshape(replicas * rows, order_size)
        matrix[...] += lax.dot_general(
            v, v, (((0,), (0,)), ((), ())), preferred_element_type=jnp.float32
        )
        return 0

    lax.fori_loop(0, micro, gather_stats, 0)
    others = old_all.at[pl.ds(0, replicas - 1)]
    old_wait = copy(others, others, old_sem.at[0], old_sem.at[1], dp=sibling)
    old_wait.wait_recv()
    scale = (1.0 - RETAIN) / (filled * (rows * replicas)).astype(jnp.float32)
    spots = lax.broadcasted_iota(jnp.int32, (order_size, order_size), 0)
    eye = spots == lax.broadcasted_iota(jnp.int32, (order_size, order_size), 1)
    full = (
        RETAIN * old_all[...].reshape(order_size, order_size)
        + scale * matrix[...]
        + jnp.where(eye, DAMPING, 0.0)
    )
    bound = jnp.max(jnp.sum(jnp.abs(full), axis=1, keepdims=True), axis=0, keepdims=True)
    unit = 1.0 / bound
    scaled = full * unit
    matrix[...] = scaled
    factor = scaled.astype(jnp.bfloat16)
    mine = lax.broadcasted_iota(jnp.int32, (band, order_size), 0) + r * band
    ones = (mine == lax.broadcasted_iota(jnp.int32, (band, order_size), 1)).astype(jnp.float32)
    total = 2.0 * ones - matrix[pl.ds(pl.multiple_of(r * band, 8), band), :]
    for _ in range(TERMS - 2):
        high = total.astype(jnp.bfloat16)
        low = (total - high.astype(jnp.float32)).astype(jnp.bfloat16)
        product = jnp.dot(high, factor, preferred_element_type=jnp.float32) + jnp.dot(
            low, factor, preferred_element_type=jnp.float32
        )
        total = ones + total - product
    inv_ref[0] = total * unit

    old_wait.wait_send()

    def drain(c, _):
        others = feats.at[c, pl.ds(0, replicas - 1)]
        copy(others, others, feat_send.at[c], feat_recv.at[c], dp=sibling).wait_send()

        @pl.when(jnp.logical_not(last))
        def _():
            copy(x_in.at[c], x_in.at[c], fwd_send.at[c], fwd_recv.at[c], section=up).wait_send()

        @pl.when(jnp.logical_not(first))
        def _():
            copy(g_in.at[c], g_in.at[c], bwd_send.at[c], bwd_recv.at[c], section=down).wait_send()

        return 0

    lax.fori_loop(0, micro, drain, 0)


def shards(sections, replicas, inputs, cotangent, weights, old_factor, plan, order):
    micro, rows, width = inputs.shape
    _, _, band, order_size = old_factor.shape
    pieces = 5 if width % 640 == 0 else width // 128
    vmem = pl.BlockSpec(memory_space=pltpu.VMEM)
    smem = pl.BlockSpec(memory_space=pltpu.SMEM)
    sems = pltpu.SemaphoreType.DMA
    zs = replicas // CORES
    return pl.pallas_call(
        functools.partial(kernel, sections, replicas, pieces),
        out_shape=(
            jax.ShapeDtypeStruct((1, micro, rows, width), jnp.bfloat16),
            jax.ShapeDtypeStruct((1, micro, rows, width), jnp.bfloat16),
            jax.ShapeDtypeStruct((1, band, order_size), jnp.float32),
        ),
        in_specs=[smem, smem, vmem, vmem, pl.BlockSpec(memory_space=pl.ANY), vmem],
        out_specs=(vmem, vmem, vmem),
        scratch_shapes=[
            pltpu.VMEM((width, width), jnp.bfloat16),
            pltpu.VMEM((width, width), jnp.bfloat16),
            pltpu.VMEM((micro, rows, width), jnp.bfloat16),
            pltpu.VMEM((micro, rows, width), jnp.bfloat16),
            pltpu.VMEM((micro, rows, width), jnp.float32),
            pltpu.VMEM((rows, width), jnp.bfloat16),
            pltpu.VMEM((micro, replicas, rows, order_size), jnp.bfloat16),
            pltpu.VMEM((replicas, band, order_size), jnp.float32),
            pltpu.VMEM((order_size, order_size), jnp.float32),
            sems,
            sems((2, zs - 1)),
            sems((2, zs - 1)),
            sems((2,)),
            sems((micro,)),
            sems((micro,)),
            sems((micro,)),
            sems((micro,)),
            sems((micro,)),
            sems((micro,)),
            sems((2,)),
        ],
        compiler_params=pltpu.CompilerParams(
            collective_id=0, has_side_effects=True, vmem_limit_bytes=56 * 2**20
        ),
    )(plan, order, inputs, cotangent, weights, old_factor)


def solution(mesh):
    return jax.shard_map(
        functools.partial(shards, mesh.shape["section"], mesh.shape["dp"]),
        mesh=mesh,
        in_specs=(
            P(None, "dp", None),
            P(None, "dp", None),
            P("section", "dp", None),
            P("section", None, "dp", None),
            P(),
            P(),
        ),
        out_specs=(
            P("section", None, "dp", None),
            P("section", None, "dp", None),
            P("section", "dp", None),
        ),
        check_vma=False,
    )
```

```python
import functools

import jax
import jax.numpy as jnp
from jax import lax
from jax.experimental import pallas as pl
from jax.experimental.pallas import tpu as pltpu
from jax.sharding import PartitionSpec as P

RETAIN = 0.6
DAMPING = 0.1
TERMS = 8
CORES = 2
BAND = 16
MESH = pl.DeviceIdType.MESH


def kernel(
    sections,
    replicas,
    pieces,
    plan_ref,
    order_ref,
    x_ref,
    ct_ref,
    w_ref,
    old_ref,
    out_ref,
    grad_ref,
    inv_ref,
    w,
    wt,
    ends,
    x_in,
    g_in,
    out,
    grad,
    slope,
    delta,
    feats,
    old_own,
    old_all,
    matrix,
    lent,
    local_sem,
    store_sem,
    ring_send,
    ring_recv,
    sib_sem,
    lend_sem,
    relay_send,
    relay_recv,
    back_send,
    back_recv,
    fwd_send,
    fwd_recv,
    bwd_send,
    bwd_recv,
    feat_send,
    feat_recv,
    feat_pass,
    feat_got,
    old_sem,
    old_pass,
):
    micro, rows, width = x_in.shape
    shard = w_ref.shape[1]
    band, order_size = old_ref.shape[2], old_ref.shape[3]
    piece = width // pieces
    zs = replicas // CORES
    lent_rows = lent.shape[1]
    bands = lent_rows // BAND
    parts = (
        (0, shard - 2 * lent_rows),
        (shard - 2 * lent_rows, lent_rows),
        (shard - lent_rows, lent_rows),
    )
    group = max(1, sections // 4)
    s = lax.axis_index("section")
    r = lax.axis_index("dp")
    z, core = r // CORES, r % CORES
    first, last = s == 0, s == sections - 1
    borrows, lends = s < group, s >= sections - group
    partner = (s + sections - group) % sections
    partner = jnp.where(borrows, partner, jnp.where(lends, s - (sections - group), s))
    sibling = z * CORES + (1 - core)
    up, down = jnp.minimum(s + 1, sections - 1), jnp.maximum(s - 1, 0)

    def along_z(steps):
        return (z + steps) % zs

    def copy(src, dst, send, recv, **device):
        return pltpu.make_async_remote_copy(
            src_ref=src,
            dst_ref=dst,
            send_sem=send,
            recv_sem=recv,
            device_id=device,
            device_id_type=MESH,
        )

    own_w = pltpu.make_async_copy(
        w_ref.at[0], w.at[pl.ds(pl.multiple_of(r * shard, 16), shard)], local_sem.at[0]
    )
    own_w.start()
    load_old = pltpu.make_async_copy(old_ref.at[0], old_own, local_sem.at[1])
    load_old.start()
    load_x = pltpu.make_async_copy(x_ref, ends, local_sem.at[2])
    load_ct = pltpu.make_async_copy(ct_ref, ends, local_sem.at[2])

    @pl.when(first)
    def _():
        load_x.start()

    @pl.when(last)
    def _():
        load_ct.start()

    barrier = pltpu.get_barrier_semaphore()

    def greet(i, _):
        there = along_z(i) * CORES + core
        pl.semaphore_signal(barrier, inc=1, device_id={"dp": there}, device_id_type=MESH)
        return 0

    lax.fori_loop(1, zs, greet, 0)
    pl.semaphore_signal(barrier, inc=1, device_id={"dp": sibling}, device_id_type=MESH)
    helped = jnp.logical_or(borrows, lends)

    @pl.when(jnp.logical_not(last))
    def _():
        pl.semaphore_signal(barrier, inc=1, device_id={"section": up}, device_id_type=MESH)

    @pl.when(jnp.logical_not(first))
    def _():
        pl.semaphore_signal(barrier, inc=1, device_id={"section": down}, device_id_type=MESH)

    @pl.when(helped)
    def _():
        pl.semaphore_signal(barrier, inc=1, device_id={"section": partner}, device_id_type=MESH)

    peers = zs + jnp.where(first, 0, 1) + jnp.where(last, 0, 1) + jnp.where(helped, 1, 0)
    pl.semaphore_wait(barrier, peers)

    def w_rows(at_z, part):
        start = (at_z * CORES + core) * shard + parts[part][0]
        return w.at[pl.ds(pl.multiple_of(start, 16), parts[part][1])]

    def own_rows(part):
        return w_ref.at[0, pl.ds(*parts[part])]

    def to_sibling(rows_there):
        copy(rows_there, rows_there, sib_sem.at[0], sib_sem.at[1], dp=sibling).start()

    def next_z(way):
        return along_z(1 if way == 0 else zs - 1) * CORES + core

    def from_z(way, hop):
        return along_z(zs - hop if way == 0 else hop)

    def hops(way, part):
        return zs // 2 if (way == 0) == (part == 0) else zs // 2 - 1

    def ring_copy(way, hop, part):
        spot = hop * 3 + part
        dst = w_rows(from_z(way, hop), part)
        src = own_rows(part) if hop == 0 else dst
        return copy(src, dst, ring_send.at[way, spot], ring_recv.at[way, spot], dp=next_z(way))

    def ring_arrival(way, hop, part):
        spot = hop * 3 + part
        here = w_rows(from_z(way, hop + 1), part)
        copy(
            here, here, ring_send.at[way, spot], ring_recv.at[way, spot], dp=next_z(way)
        ).wait_recv()
        return here

    def lent_band(at_z, i):
        return lent.at[at_z, pl.ds(i * BAND, BAND)]

    def lend(i):
        start = parts[2][0] + i * BAND
        return copy(
            w_ref.at[0, pl.ds(start, BAND)],
            lent_band(z, i),
            lend_sem.at[0, i],
            lend_sem.at[1, i],
            section=partner,
        )

    def relay_copy(way, hop, i, at=0):
        here = lent_band(from_z(way, hop + at), i)
        return copy(
            here, here, relay_send.at[way, hop, i], relay_recv.at[way, hop, i], dp=next_z(way)
        )

    def give_back(way, hop, i):
        at_z = from_z(way, hop + 1)
        start = (at_z * CORES + core) * shard + parts[2][0] + i * BAND
        return copy(
            lent_band(at_z, i),
            w.at[pl.ds(pl.multiple_of(start, 16), BAND)],
            back_send.at[way, hop, i],
            back_recv.at[way, hop, i],
            section=partner,
        )

    def back_arrival(way, hop):
        for i in range(bands):
            give_back(way, hop, i).wait_recv()
        to_sibling(w_rows(from_z(way, hop + 1), 2))

    lent_hops = (zs // 2, zs // 2 - 1)

    def ring(some_parts, extra):
        for hop in range(zs // 2 + 1):
            for part in some_parts:
                for way in range(2):
                    came = None
                    if 0 < hop <= hops(way, part):
                        came = ring_arrival(way, hop - 1, part)
                    if hop < hops(way, part):
                        ring_copy(way, hop, part).start()
                    if came is not None:
                        to_sibling(came)
            if hop == 0:
                own_w.wait()
                to_sibling(w.at[pl.ds(pl.multiple_of(r * shard, 16), shard)])
            if hop >= 2:
                extra(hop - 2)
        extra(zs // 2 - 1)

    @pl.when(borrows)
    def _():
        for i in range(bands):
            lend(i).start()

        def extra(hop):
            for way in range(2):
                if hop < lent_hops[way]:
                    back_arrival(way, hop)

        ring((0, 1), extra)

    @pl.when(lends)
    def _():
        for hop in range(zs // 2 + 1):
            for i in range(bands):
                if hop == 0:
                    lend(i).wait_recv()
                for way in range(2):
                    came = 0 < hop <= lent_hops[way]
                    if came:
                        relay_copy(way, hop - 1, i, 1).wait_recv()
                    if hop < lent_hops[way]:
                        relay_copy(way, hop, i).start()
                    if came:
                        give_back(way, hop - 1, i).start()

    @pl.when(jnp.logical_not(borrows))
    def _():
        ring((0, 1, 2), lambda hop: None)

    load_old.wait()
    block = plan_ref[0, s]
    filled = plan_ref[2, s]
    old_all[z, core] = old_own[block]

    def send_old(i, _):
        here = old_all.at[z, core]
        copy(here, here, old_sem.at[0], old_sem.at[1], dp=along_z(i) * CORES + core).start()
        return 0

    lax.fori_loop(1, zs, send_old, 0)
    all_sib = w.at[pl.ds(0, zs * shard)]
    sib_wait = copy(all_sib, all_sib, sib_sem.at[0], sib_sem.at[1], dp=sibling)
    sib_wait.wait_recv()

    def turn_weights():
        tile = 2 * 128
        spots = lax.broadcasted_iota(jnp.int32, (tile, tile), 0)
        eye = (spots == lax.broadcasted_iota(jnp.int32, (tile, tile), 1)).astype(jnp.bfloat16)

        def turn(i, _):
            at = pl.ds(pl.multiple_of(i * tile, tile), tile)
            for j in range(pieces):
                cols = pl.ds(j * piece, piece)
                wt[cols, at] = lax.dot_general(
                    w[at, cols], eye, (((0,), (0,)), ((), ())), preferred_element_type=jnp.float32
                ).astype(jnp.bfloat16)
            return 0

        lax.fori_loop(0, width // tile, turn, 0)

    def store(ref, c, whole_ref, sem):
        return pltpu.make_async_copy(ref.at[c], whole_ref.at[0, c], sem)

    def forward(c, count, sends):
        for i in range(count):
            arrival = copy(
                x_in.at[c + i], x_in.at[c + i], fwd_send.at[c + i], fwd_recv.at[c + i], section=up
            )
            if sends:

                @pl.when(first)
                def _():
                    x_in[c + i] = ends[order_ref[c + i]]

                @pl.when(jnp.logical_not(first))
                def _():
                    arrival.wait_recv()

            else:
                arrival.wait_recv()

        these = pl.ds(c, count)
        x = x_in[these].reshape(count * rows, width)
        for j in range(pieces):
            cols = pl.ds(j * piece, piece)
            pre = jnp.dot(x, w[:, cols], preferred_element_type=jnp.float32)
            pre = pre.reshape(count, rows, piece)
            gate = jax.nn.sigmoid(pre)
            out[these, :, cols] = (x_in[these, :, cols].astype(jnp.float32) + pre * gate).astype(
                jnp.bfloat16
            )
            if sends:
                copy(
                    out.at[c, :, cols],
                    x_in.at[c, :, cols],
                    fwd_send.at[c],
                    fwd_recv.at[c],
                    section=up,
                ).start()
            slope[these, :, cols] = gate * (1.0 + pre * (1.0 - gate))
        for i in range(count):
            store(out, c + i, out_ref, store_sem.at[0, c + i]).start()

    def forward_step(c, _):
        forward(c, 1, True)
        return 0

    @pl.when(first)
    def _():
        load_x.wait()

    @pl.when(jnp.logical_not(last))
    def _():
        lax.fori_loop(0, micro, forward_step, 0)

    turn_weights()

    own_old = old_all.at[:, core]
    some_old = old_all.at[pl.ds(0, zs - 1), core]
    copy(some_old, some_old, old_sem.at[0], old_sem.at[1], dp=sibling).wait_recv()
    pass_old = copy(own_old, own_old, old_pass.at[0], old_pass.at[1], dp=sibling)
    pass_old.start()
    matrix[...] = jnp.zeros_like(matrix)
    place = block % (width // order_size)
    from_input = block < width // order_size

    def gradient_in(c):
        @pl.when(last)
        def _():
            g_in[c] = ends[order_ref[c]]

        @pl.when(jnp.logical_not(last))
        def _():
            copy(g_in.at[c], g_in.at[c], bwd_send.at[c], bwd_recv.at[c], section=down).wait_recv()

        delta[c] = (g_in[c].astype(jnp.float32) * slope[c]).astype(jnp.bfloat16)

    def share_features(c):
        chosen = jnp.zeros((rows, order_size), jnp.bfloat16)
        for j in range(width // order_size):
            cols = pl.ds(j * order_size, order_size)
            here = jnp.where(from_input, x_in[c, :, cols], delta[c, :, cols])
            chosen = jnp.where(place == j, here, chosen)
        feats[c, core, z] = jnp.where(c < filled, chosen, jnp.zeros_like(chosen))

        def send_feats(i, _):
            here = feats.at[c, core, z]
            there = along_z(i) * CORES + core
            copy(here, here, feat_send.at[c], feat_recv.at[c], dp=there).start()
            return 0

        lax.fori_loop(1, zs, send_feats, 0)

    def feats_in(c):
        some = feats.at[c, core, pl.ds(0, zs - 1)]
        return copy(some, some, feat_send.at[c], feat_recv.at[c], dp=sibling)

    def feats_pass(c):
        here = feats.at[c, core]
        return copy(here, here, feat_pass.at[c], feat_got.at[c], dp=sibling)

    def pass_features(c, _=0):
        feats_in(c).wait_recv()
        feats_pass(c).start()
        return 0

    def add_stats(c, _=0):
        feats_pass(c).wait_recv()
        v = feats[c].reshape(replicas * rows, order_size)
        matrix[...] += lax.dot_general(
            v, v, (((0,), (0,)), ((), ())), preferred_element_type=jnp.float32
        )
        return 0

    def backward(c, count):
        for i in range(count):
            gradient_in(c + i)
        these = pl.ds(c, count)
        d = delta[these].reshape(count * rows, width)
        for j in range(pieces):
            cols = pl.ds(j * piece, piece)
            back = jnp.dot(d, wt[:, cols], preferred_element_type=jnp.float32)
            back = back.reshape(count, rows, piece)
            grad[these, :, cols] = (g_in[these, :, cols].astype(jnp.float32) + back).astype(
                jnp.bfloat16
            )
            copy(
                grad.at[c, :, cols],
                g_in.at[c, :, cols],
                bwd_send.at[c],
                bwd_recv.at[c],
                section=down,
            ).start()
        for i in range(1, count):
            copy(
                grad.at[c + i], g_in.at[c + i], bwd_send.at[c + i], bwd_recv.at[c + i], section=down
            ).start()
        for i in range(count):
            share_features(c + i)
            store(grad, c + i, grad_ref, store_sem.at[1, c + i]).start()

    def backward_step(c, _):
        backward(c, 1)
        return 0

    @pl.when(jnp.logical_not(jnp.logical_or(first, last)))
    def _():
        lax.fori_loop(0, micro, backward_step, 0)

    @pl.when(last)
    def _():
        load_ct.wait()

        def turn_round(c, count):
            forward(c, count, False)
            backward(c, count)

        def by_twos(i, _):
            turn_round(1 + 2 * i, 2)
            return 0

        turn_round(0, 1)
        lax.fori_loop(0, (micro - 2) // 2, by_twos, 0)
        turn_round(micro - 1, 1)

    @pl.when(jnp.logical_not(first))
    def _():
        lax.fori_loop(0, micro, pass_features, 0)
        lax.fori_loop(0, micro, add_stats, 0)

    lag = min(3, micro - 1)

    def backward_first(c, _):
        gradient_in(c)
        share_features(c)

        @pl.when(c >= lag)
        def _():
            pass_features(c - lag)

        @pl.when(c > lag)
        def _():
            add_stats(c - lag - 1)

        return 0

    @pl.when(first)
    def _():
        lax.fori_loop(0, micro, backward_first, 0)
        lax.fori_loop(micro - lag, micro - 1, pass_features, 0)
        add_stats(micro - lag - 1)

        def all_gradients(j, _):
            cols = pl.ds(pl.multiple_of(j * piece, 128), piece)
            d = delta[...].reshape(micro * rows, width)
            back = jnp.dot(d, wt[:, cols], preferred_element_type=jnp.float32)
            total = g_in[:, :, cols].astype(jnp.float32) + back.reshape(micro, rows, piece)
            grad[:, :, cols] = total.astype(jnp.bfloat16)
            return 0

        lax.fori_loop(0, pieces, all_gradients, 0)

        def store_all(c, _):
            store(grad, c, grad_ref, store_sem.at[1, c]).start()
            return 0

        lax.fori_loop(0, micro, store_all, 0)
        lax.fori_loop(micro - lag, micro - 1, add_stats, 0)
        pass_features(micro - 1)
        add_stats(micro - 1)

    pass_old.wait_recv()
    scale = (1.0 - RETAIN) / (filled * (rows * replicas)).astype(jnp.float32)
    spots = lax.broadcasted_iota(jnp.int32, (order_size, order_size), 0)
    eye = spots == lax.broadcasted_iota(jnp.int32, (order_size, order_size), 1)
    full = (
        RETAIN * old_all[...].reshape(order_size, order_size)
        + scale * matrix[...]
        + jnp.where(eye, DAMPING, 0.0)
    )
    bound = jnp.max(jnp.sum(jnp.abs(full), axis=1, keepdims=True), axis=0, keepdims=True)
    unit = 1.0 / bound
    scaled = full * unit
    matrix[...] = scaled
    factor = scaled.astype(jnp.bfloat16)
    row_ids = lax.broadcasted_iota(jnp.int32, (band, order_size), 0) + r * band
    ones = (row_ids == lax.broadcasted_iota(jnp.int32, (band, order_size), 1)).astype(jnp.float32)
    total = 2.0 * ones - matrix[pl.ds(pl.multiple_of(r * band, 8), band), :]
    for _ in range(TERMS - 2):
        high = total.astype(jnp.bfloat16)
        low = (total - high.astype(jnp.float32)).astype(jnp.bfloat16)
        product = jnp.dot(high, factor, preferred_element_type=jnp.float32) + jnp.dot(
            low, factor, preferred_element_type=jnp.float32
        )
        total = ones + total - product
    inv_ref[0] = total * unit

    def drain_ring(some_parts):
        for part in some_parts:
            for way in range(2):
                for hop in range(hops(way, part)):
                    ring_copy(way, hop, part).wait_send()

    drain_ring((0, 1))

    @pl.when(borrows)
    def _():
        for i in range(bands):
            lend(i).wait_send()

    @pl.when(jnp.logical_not(borrows))
    def _():
        drain_ring((2,))

    @pl.when(lends)
    def _():
        for way in range(2):
            for hop in range(lent_hops[way]):
                for i in range(bands):
                    relay_copy(way, hop, i).wait_send()
                    give_back(way, hop, i).wait_send()

    sib_wait.wait_send()
    copy(some_old, some_old, old_sem.at[0], old_sem.at[1], dp=sibling).wait_send()
    pass_old.wait_send()

    def drain(c, _):
        feats_in(c).wait_send()
        feats_pass(c).wait_send()
        store(out, c, out_ref, store_sem.at[0, c]).wait()
        store(grad, c, grad_ref, store_sem.at[1, c]).wait()

        @pl.when(jnp.logical_not(last))
        def _():
            copy(out.at[c], x_in.at[c], fwd_send.at[c], fwd_recv.at[c], section=up).wait_send()

        @pl.when(jnp.logical_not(first))
        def _():
            copy(grad.at[c], g_in.at[c], bwd_send.at[c], bwd_recv.at[c], section=down).wait_send()

        return 0

    lax.fori_loop(0, micro, drain, 0)


def shards(sections, replicas, inputs, cotangent, weights, old_factor, plan, order):
    micro, rows, width = inputs.shape
    _, blocks, band, order_size = old_factor.shape
    shard = weights.shape[1]
    lent_rows = shard // 16 * 3 // 10 * 16
    pieces = 5 if width % 640 == 0 else width // 128
    vmem = pl.BlockSpec(memory_space=pltpu.VMEM)
    smem = pl.BlockSpec(memory_space=pltpu.SMEM)
    free = pl.BlockSpec(memory_space=pl.ANY)
    hbm = pl.BlockSpec(memory_space=pltpu.HBM)
    sems = pltpu.SemaphoreType.DMA
    zs = replicas // CORES
    acts = pltpu.VMEM((micro, rows, width), jnp.bfloat16)
    return pl.pallas_call(
        functools.partial(kernel, sections, replicas, pieces),
        out_shape=(
            jax.ShapeDtypeStruct((1, micro, rows, width), jnp.bfloat16),
            jax.ShapeDtypeStruct((1, micro, rows, width), jnp.bfloat16),
            jax.ShapeDtypeStruct((1, band, order_size), jnp.float32),
        ),
        in_specs=[smem, smem, hbm, hbm, hbm, hbm],
        out_specs=(free, free, vmem),
        scratch_shapes=[
            pltpu.VMEM((width, width), jnp.bfloat16),
            pltpu.VMEM((width, width), jnp.bfloat16),
            acts,
            acts,
            acts,
            acts,
            acts,
            pltpu.VMEM((micro, rows, width), jnp.float32),
            acts,
            pltpu.VMEM((micro, CORES, zs, rows, order_size), jnp.bfloat16),
            pltpu.VMEM((blocks, band, order_size), jnp.float32),
            pltpu.VMEM((zs, CORES, band, order_size), jnp.float32),
            pltpu.VMEM((order_size, order_size), jnp.float32),
            pltpu.VMEM((zs, lent_rows, width), jnp.bfloat16),
            sems((3,)),
            sems((2, micro)),
            sems((2, 3 * (zs // 2))),
            sems((2, 3 * (zs // 2))),
            sems((2,)),
            sems((2, lent_rows // BAND)),
            sems((2, zs // 2, lent_rows // BAND)),
            sems((2, zs // 2, lent_rows // BAND)),
            sems((2, zs // 2, lent_rows // BAND)),
            sems((2, zs // 2, lent_rows // BAND)),
            sems((micro,)),
            sems((micro,)),
            sems((micro,)),
            sems((micro,)),
            sems((micro,)),
            sems((micro,)),
            sems((micro,)),
            sems((micro,)),
            sems((2,)),
            sems((2,)),
        ],
        compiler_params=pltpu.CompilerParams(
            collective_id=0, has_side_effects=True, vmem_limit_bytes=52 * 2**20
        ),
    )(plan.T, order, inputs, cotangent, weights, old_factor)


def solution(mesh):
    return jax.shard_map(
        functools.partial(shards, mesh.shape["section"], mesh.shape["dp"]),
        mesh=mesh,
        in_specs=(
            P(None, "dp", None),
            P(None, "dp", None),
            P("section", "dp", None),
            P("section", None, "dp", None),
            P(),
            P(),
        ),
        out_specs=(
            P("section", None, "dp", None),
            P("section", None, "dp", None),
            P("section", "dp", None),
        ),
        check_vma=False,
    )
```

```python
import functools

import jax
import jax.numpy as jnp
from jax import lax
from jax.experimental import pallas as pl
from jax.experimental.pallas import tpu as pltpu
from jax.sharding import PartitionSpec as P

RETAIN = 0.6
DAMPING = 0.1
TERMS = 8
CORES = 2
BAND = 16
MESH = pl.DeviceIdType.MESH


def kernel(
    sections,
    replicas,
    pieces,
    plan_ref,
    order_ref,
    x_ref,
    ct_ref,
    w_ref,
    old_ref,
    out_ref,
    grad_ref,
    inv_ref,
    w,
    wt,
    ends,
    x_in,
    g_in,
    out,
    grad,
    slope,
    delta,
    feats,
    old_own,
    old_all,
    matrix,
    lent,
    local_sem,
    store_sem,
    ring_send,
    ring_recv,
    sib_sem,
    lend_sem,
    relay_send,
    relay_recv,
    back_send,
    back_recv,
    fwd_send,
    fwd_recv,
    bwd_send,
    bwd_recv,
    feat_send,
    feat_recv,
    feat_pass,
    feat_got,
    old_sem,
    old_pass,
):
    micro, rows, width = x_in.shape
    shard = w_ref.shape[1]
    band, order_size = old_ref.shape[2], old_ref.shape[3]
    piece = width // pieces
    zs = replicas // CORES
    lent_rows = lent.shape[1]
    bands = lent_rows // BAND
    parts = (
        (0, shard - 2 * lent_rows),
        (shard - 2 * lent_rows, lent_rows),
        (shard - lent_rows, lent_rows),
    )
    group = max(1, sections // 4)
    s = lax.axis_index("section")
    r = lax.axis_index("dp")
    z, core = r // CORES, r % CORES
    first, last = s == 0, s == sections - 1
    borrows, lends = s < group, s >= sections - group
    partner = (s + sections - group) % sections
    partner = jnp.where(borrows, partner, jnp.where(lends, s - (sections - group), s))
    sibling = z * CORES + (1 - core)
    up, down = jnp.minimum(s + 1, sections - 1), jnp.maximum(s - 1, 0)

    def along_z(steps):
        return (z + steps) % zs

    def copy(src, dst, send, recv, **device):
        return pltpu.make_async_remote_copy(
            src_ref=src,
            dst_ref=dst,
            send_sem=send,
            recv_sem=recv,
            device_id=device,
            device_id_type=MESH,
        )

    own_w = pltpu.make_async_copy(
        w_ref.at[0], w.at[pl.ds(pl.multiple_of(r * shard, 16), shard)], local_sem.at[0]
    )
    own_w.start()
    load_old = pltpu.make_async_copy(old_ref.at[0], old_own, local_sem.at[1])
    load_old.start()
    load_x = pltpu.make_async_copy(x_ref, ends, local_sem.at[2])
    load_ct = pltpu.make_async_copy(ct_ref, ends, local_sem.at[2])

    @pl.when(first)
    def _():
        load_x.start()

    @pl.when(last)
    def _():
        load_ct.start()

    barrier = pltpu.get_barrier_semaphore()

    def greet(i, _):
        there = along_z(i) * CORES + core
        pl.semaphore_signal(barrier, inc=1, device_id={"dp": there}, device_id_type=MESH)
        return 0

    lax.fori_loop(1, zs, greet, 0)
    pl.semaphore_signal(barrier, inc=1, device_id={"dp": sibling}, device_id_type=MESH)
    helped = jnp.logical_or(borrows, lends)

    @pl.when(jnp.logical_not(last))
    def _():
        pl.semaphore_signal(barrier, inc=1, device_id={"section": up}, device_id_type=MESH)

    @pl.when(jnp.logical_not(first))
    def _():
        pl.semaphore_signal(barrier, inc=1, device_id={"section": down}, device_id_type=MESH)

    @pl.when(helped)
    def _():
        pl.semaphore_signal(barrier, inc=1, device_id={"section": partner}, device_id_type=MESH)

    peers = zs + jnp.where(first, 0, 1) + jnp.where(last, 0, 1) + jnp.where(helped, 1, 0)
    pl.semaphore_wait(barrier, peers)

    def w_rows(at_z, part):
        start = (at_z * CORES + core) * shard + parts[part][0]
        return w.at[pl.ds(pl.multiple_of(start, 16), parts[part][1])]

    def own_rows(part):
        return w_ref.at[0, pl.ds(*parts[part])]

    def to_sibling(rows_there):
        copy(rows_there, rows_there, sib_sem.at[0], sib_sem.at[1], dp=sibling).start()

    def next_z(way):
        return along_z(1 if way == 0 else zs - 1) * CORES + core

    def from_z(way, hop):
        return along_z(zs - hop if way == 0 else hop)

    def hops(way, part):
        return zs // 2 if (way == 0) == (part == 0) else zs // 2 - 1

    def ring_copy(way, hop, part):
        spot = hop * 3 + part
        dst = w_rows(from_z(way, hop), part)
        src = own_rows(part) if hop == 0 else dst
        return copy(src, dst, ring_send.at[way, spot], ring_recv.at[way, spot], dp=next_z(way))

    def ring_arrival(way, hop, part):
        spot = hop * 3 + part
        here = w_rows(from_z(way, hop + 1), part)
        copy(
            here, here, ring_send.at[way, spot], ring_recv.at[way, spot], dp=next_z(way)
        ).wait_recv()
        return here

    def lent_band(at_z, i):
        return lent.at[at_z, pl.ds(i * BAND, BAND)]

    def lend(i):
        start = parts[2][0] + i * BAND
        return copy(
            w_ref.at[0, pl.ds(start, BAND)],
            lent_band(z, i),
            lend_sem.at[0, i],
            lend_sem.at[1, i],
            section=partner,
        )

    def relay_copy(way, hop, i, at=0):
        here = lent_band(from_z(way, hop + at), i)
        return copy(
            here, here, relay_send.at[way, hop, i], relay_recv.at[way, hop, i], dp=next_z(way)
        )

    def give_back(way, hop, i):
        at_z = from_z(way, hop + 1)
        start = (at_z * CORES + core) * shard + parts[2][0] + i * BAND
        return copy(
            lent_band(at_z, i),
            w.at[pl.ds(pl.multiple_of(start, 16), BAND)],
            back_send.at[way, hop, i],
            back_recv.at[way, hop, i],
            section=partner,
        )

    def back_arrival(way, hop):
        for i in range(bands):
            give_back(way, hop, i).wait_recv()
        to_sibling(w_rows(from_z(way, hop + 1), 2))

    lent_hops = (zs // 2, zs // 2 - 1)

    def ring(some_parts, extra):
        for hop in range(zs // 2 + 1):
            for part in some_parts:
                for way in range(2):
                    came = None
                    if 0 < hop <= hops(way, part):
                        came = ring_arrival(way, hop - 1, part)
                    if hop < hops(way, part):
                        ring_copy(way, hop, part).start()
                    if came is not None:
                        to_sibling(came)
            if hop == 0:
                own_w.wait()
                to_sibling(w.at[pl.ds(pl.multiple_of(r * shard, 16), shard)])
            if hop >= 2:
                extra(hop - 2)
        extra(zs // 2 - 1)

    @pl.when(borrows)
    def _():
        for i in range(bands):
            lend(i).start()

        def extra(hop):
            for way in range(2):
                if hop < lent_hops[way]:
                    back_arrival(way, hop)

        ring((0, 1), extra)

    @pl.when(lends)
    def _():
        for hop in range(zs // 2 + 1):
            for i in range(bands):
                if hop == 0:
                    lend(i).wait_recv()
                for way in range(2):
                    came = 0 < hop <= lent_hops[way]
                    if came:
                        relay_copy(way, hop - 1, i, 1).wait_recv()
                    if hop < lent_hops[way]:
                        relay_copy(way, hop, i).start()
                    if came:
                        give_back(way, hop - 1, i).start()

    @pl.when(jnp.logical_not(borrows))
    def _():
        ring((0, 1, 2), lambda hop: None)

    load_old.wait()
    block = plan_ref[0, s]
    filled = plan_ref[2, s]
    old_all[z, core] = old_own[block]

    def send_old(i, _):
        here = old_all.at[z, core]
        copy(here, here, old_sem.at[0], old_sem.at[1], dp=along_z(i) * CORES + core).start()
        return 0

    lax.fori_loop(1, zs, send_old, 0)
    all_sib = w.at[pl.ds(0, zs * shard)]
    sib_wait = copy(all_sib, all_sib, sib_sem.at[0], sib_sem.at[1], dp=sibling)
    sib_wait.wait_recv()

    def turn_weights():
        tile = 2 * 128
        spots = lax.broadcasted_iota(jnp.int32, (tile, tile), 0)
        eye = (spots == lax.broadcasted_iota(jnp.int32, (tile, tile), 1)).astype(jnp.bfloat16)

        def turn(i, _):
            at = pl.ds(pl.multiple_of(i * tile, tile), tile)
            for j in range(pieces):
                cols = pl.ds(j * piece, piece)
                wt[cols, at] = lax.dot_general(
                    w[at, cols], eye, (((0,), (0,)), ((), ())), preferred_element_type=jnp.float32
                ).astype(jnp.bfloat16)
            return 0

        lax.fori_loop(0, width // tile, turn, 0)

    def store(ref, c, whole_ref, sem):
        return pltpu.make_async_copy(ref.at[c], whole_ref.at[0, c], sem)

    def by_pieces(value, matrix_ref, finish):
        before = None
        for j in range(pieces):
            cols = pl.ds(j * piece, piece)
            product = jnp.dot(value, matrix_ref[:, cols], preferred_element_type=jnp.float32)
            if before is not None:
                finish(*before)
            before = (cols, product)
        finish(*before)

    def forward(c, count, sends):
        for i in range(count):
            arrival = copy(
                x_in.at[c + i], x_in.at[c + i], fwd_send.at[c + i], fwd_recv.at[c + i], section=up
            )
            if sends:

                @pl.when(first)
                def _():
                    x_in[c + i] = ends[order_ref[c + i]]

                @pl.when(jnp.logical_not(first))
                def _():
                    arrival.wait_recv()

            else:
                arrival.wait_recv()

        these = pl.ds(c, count)
        x = x_in[these].reshape(count * rows, width)

        def finish(cols, pre):
            pre = pre.reshape(count, rows, piece)
            gate = jax.nn.sigmoid(pre)
            out[these, :, cols] = (x_in[these, :, cols].astype(jnp.float32) + pre * gate).astype(
                jnp.bfloat16
            )
            if sends:
                copy(
                    out.at[c, :, cols],
                    x_in.at[c, :, cols],
                    fwd_send.at[c],
                    fwd_recv.at[c],
                    section=up,
                ).start()
            slope[these, :, cols] = gate * (1.0 + pre * (1.0 - gate))

        by_pieces(x, w, finish)
        for i in range(count):
            store(out, c + i, out_ref, store_sem.at[0, c + i]).start()

    def forward_step(c, _):
        forward(c, 1, True)
        return 0

    @pl.when(first)
    def _():
        load_x.wait()

    @pl.when(s >= sections // 2)
    def _():
        turn_weights()

    @pl.when(jnp.logical_not(last))
    def _():
        lax.fori_loop(0, micro, forward_step, 0)

    @pl.when(s < sections // 2)
    def _():
        turn_weights()

    own_old = old_all.at[:, core]
    some_old = old_all.at[pl.ds(0, zs - 1), core]
    copy(some_old, some_old, old_sem.at[0], old_sem.at[1], dp=sibling).wait_recv()
    pass_old = copy(own_old, own_old, old_pass.at[0], old_pass.at[1], dp=sibling)
    pass_old.start()
    pass_old.wait_recv()
    scale = (1.0 - RETAIN) / (filled * (rows * replicas)).astype(jnp.float32)
    spots = lax.broadcasted_iota(jnp.int32, (order_size, order_size), 0)
    eye = spots == lax.broadcasted_iota(jnp.int32, (order_size, order_size), 1)
    matrix[...] = RETAIN * old_all[...].reshape(order_size, order_size) + jnp.where(
        eye, DAMPING, 0.0
    )
    place = block % (width // order_size)
    from_input = block < width // order_size

    def gradient_in(c):
        @pl.when(last)
        def _():
            g_in[c] = ends[order_ref[c]]

        @pl.when(jnp.logical_not(last))
        def _():
            copy(g_in.at[c], g_in.at[c], bwd_send.at[c], bwd_recv.at[c], section=down).wait_recv()

        delta[c] = (g_in[c].astype(jnp.float32) * slope[c]).astype(jnp.bfloat16)

    def share_features(c):
        chosen = jnp.zeros((rows, order_size), jnp.bfloat16)
        for j in range(width // order_size):
            cols = pl.ds(j * order_size, order_size)
            here = jnp.where(from_input, x_in[c, :, cols], delta[c, :, cols])
            chosen = jnp.where(place == j, here, chosen)
        feats[c, core, z] = jnp.where(c < filled, chosen, jnp.zeros_like(chosen))

        for i in sorted(range(1, zs), key=lambda i: -min(i, zs - i)):
            here = feats.at[c, core, z]
            there = along_z(i) * CORES + core
            copy(here, here, feat_send.at[c], feat_recv.at[c], dp=there).start()

    def feats_in(c):
        some = feats.at[c, core, pl.ds(0, zs - 1)]
        return copy(some, some, feat_send.at[c], feat_recv.at[c], dp=sibling)

    def feats_pass(c):
        here = feats.at[c, core]
        return copy(here, here, feat_pass.at[c], feat_got.at[c], dp=sibling)

    def pass_features(c, _=0):
        feats_in(c).wait_recv()
        feats_pass(c).start()
        return 0

    def add_stats(c, _=0):
        feats_pass(c).wait_recv()
        v = feats[c].reshape(replicas * rows, order_size)
        matrix[...] += scale * lax.dot_general(
            v, v, (((0,), (0,)), ((), ())), preferred_element_type=jnp.float32
        )
        return 0

    def backward(c, count):
        for i in range(count):
            gradient_in(c + i)
        these = pl.ds(c, count)
        d = delta[these].reshape(count * rows, width)

        def finish(cols, back):
            back = back.reshape(count, rows, piece)
            grad[these, :, cols] = (g_in[these, :, cols].astype(jnp.float32) + back).astype(
                jnp.bfloat16
            )
            copy(
                grad.at[c, :, cols],
                g_in.at[c, :, cols],
                bwd_send.at[c],
                bwd_recv.at[c],
                section=down,
            ).start()

        by_pieces(d, wt, finish)
        for i in range(1, count):
            copy(
                grad.at[c + i], g_in.at[c + i], bwd_send.at[c + i], bwd_recv.at[c + i], section=down
            ).start()
        for i in range(count):
            share_features(c + i)
            store(grad, c + i, grad_ref, store_sem.at[1, c + i]).start()

    def backward_step(c, _):
        backward(c, 1)
        return 0

    @pl.when(jnp.logical_not(jnp.logical_or(first, last)))
    def _():
        lax.fori_loop(0, micro, backward_step, 0)

    @pl.when(last)
    def _():
        load_ct.wait()

        def turn_round(c, count):
            forward(c, count, False)
            backward(c, count)

        def by_twos(i, _):
            turn_round(1 + 2 * i, 2)
            return 0

        turn_round(0, 1)
        lax.fori_loop(0, (micro - 2) // 2, by_twos, 0)
        turn_round(micro - 1, 1)

    @pl.when(jnp.logical_not(first))
    def _():
        lax.fori_loop(0, micro, pass_features, 0)
        lax.fori_loop(0, micro, add_stats, 0)

    lag = min(3, micro - 1)

    def backward_first(c, _):
        gradient_in(c)
        share_features(c)

        @pl.when(c >= lag)
        def _():
            pass_features(c - lag)

        @pl.when(c > lag)
        def _():
            add_stats(c - lag - 1)

        return 0

    @pl.when(first)
    def _():
        lax.fori_loop(0, micro, backward_first, 0)
        lax.fori_loop(micro - lag, micro - 1, pass_features, 0)
        add_stats(micro - lag - 1)

        def all_gradients(j, _):
            cols = pl.ds(pl.multiple_of(j * piece, 128), piece)
            d = delta[...].reshape(micro * rows, width)
            back = jnp.dot(d, wt[:, cols], preferred_element_type=jnp.float32)
            total = g_in[:, :, cols].astype(jnp.float32) + back.reshape(micro, rows, piece)
            grad[:, :, cols] = total.astype(jnp.bfloat16)
            return 0

        lax.fori_loop(0, pieces, all_gradients, 0)

        def store_all(c, _):
            store(grad, c, grad_ref, store_sem.at[1, c]).start()
            return 0

        lax.fori_loop(0, micro, store_all, 0)
        lax.fori_loop(micro - lag, micro - 1, add_stats, 0)
        pass_features(micro - 1)
        add_stats(micro - 1)

    full = matrix[...]
    bound = jnp.max(jnp.sum(jnp.abs(full), axis=1, keepdims=True), axis=0, keepdims=True)
    unit = 1.0 / bound
    factor = (full * unit).astype(jnp.bfloat16)
    row_ids = lax.broadcasted_iota(jnp.int32, (band, order_size), 0) + r * band
    ones = (row_ids == lax.broadcasted_iota(jnp.int32, (band, order_size), 1)).astype(jnp.float32)
    total = 2.0 * ones - matrix[pl.ds(pl.multiple_of(r * band, 8), band), :] * unit
    for _ in range(TERMS - 2):
        product = jnp.dot(
            total.astype(jnp.bfloat16), factor, preferred_element_type=jnp.float32
        )
        total = ones + total - product
    inv_ref[0] = total * unit

    def drain_ring(some_parts):
        for part in some_parts:
            for way in range(2):
                for hop in range(hops(way, part)):
                    ring_copy(way, hop, part).wait_send()

    drain_ring((0, 1))

    @pl.when(borrows)
    def _():
        for i in range(bands):
            lend(i).wait_send()

    @pl.when(jnp.logical_not(borrows))
    def _():
        drain_ring((2,))

    @pl.when(lends)
    def _():
        for way in range(2):
            for hop in range(lent_hops[way]):
                for i in range(bands):
                    relay_copy(way, hop, i).wait_send()
                    give_back(way, hop, i).wait_send()

    sib_wait.wait_send()
    copy(some_old, some_old, old_sem.at[0], old_sem.at[1], dp=sibling).wait_send()
    pass_old.wait_send()

    def drain(c, _):
        feats_in(c).wait_send()
        feats_pass(c).wait_send()
        store(out, c, out_ref, store_sem.at[0, c]).wait()
        store(grad, c, grad_ref, store_sem.at[1, c]).wait()

        @pl.when(jnp.logical_not(last))
        def _():
            copy(out.at[c], x_in.at[c], fwd_send.at[c], fwd_recv.at[c], section=up).wait_send()

        @pl.when(jnp.logical_not(first))
        def _():
            copy(grad.at[c], g_in.at[c], bwd_send.at[c], bwd_recv.at[c], section=down).wait_send()

        return 0

    lax.fori_loop(0, micro, drain, 0)


def shards(sections, replicas, inputs, cotangent, weights, old_factor, plan, order):
    micro, rows, width = inputs.shape
    _, blocks, band, order_size = old_factor.shape
    shard = weights.shape[1]
    lent_rows = shard // 16 * 3 // 10 * 16
    pieces = 5 if width % 640 == 0 else width // 128
    vmem = pl.BlockSpec(memory_space=pltpu.VMEM)
    smem = pl.BlockSpec(memory_space=pltpu.SMEM)
    free = pl.BlockSpec(memory_space=pl.ANY)
    hbm = pl.BlockSpec(memory_space=pltpu.HBM)
    sems = pltpu.SemaphoreType.DMA
    zs = replicas // CORES
    acts = pltpu.VMEM((micro, rows, width), jnp.bfloat16)
    return pl.pallas_call(
        functools.partial(kernel, sections, replicas, pieces),
        out_shape=(
            jax.ShapeDtypeStruct((1, micro, rows, width), jnp.bfloat16),
            jax.ShapeDtypeStruct((1, micro, rows, width), jnp.bfloat16),
            jax.ShapeDtypeStruct((1, band, order_size), jnp.float32),
        ),
        in_specs=[smem, smem, hbm, hbm, hbm, hbm],
        out_specs=(free, free, vmem),
        scratch_shapes=[
            pltpu.VMEM((width, width), jnp.bfloat16),
            pltpu.VMEM((width, width), jnp.bfloat16),
            acts,
            acts,
            acts,
            acts,
            acts,
            pltpu.VMEM((micro, rows, width), jnp.float32),
            acts,
            pltpu.VMEM((micro, CORES, zs, rows, order_size), jnp.bfloat16),
            pltpu.VMEM((blocks, band, order_size), jnp.float32),
            pltpu.VMEM((zs, CORES, band, order_size), jnp.float32),
            pltpu.VMEM((order_size, order_size), jnp.float32),
            pltpu.VMEM((zs, lent_rows, width), jnp.bfloat16),
            sems((3,)),
            sems((2, micro)),
            sems((2, 3 * (zs // 2))),
            sems((2, 3 * (zs // 2))),
            sems((2,)),
            sems((2, lent_rows // BAND)),
            sems((2, zs // 2, lent_rows // BAND)),
            sems((2, zs // 2, lent_rows // BAND)),
            sems((2, zs // 2, lent_rows // BAND)),
            sems((2, zs // 2, lent_rows // BAND)),
            sems((micro,)),
            sems((micro,)),
            sems((micro,)),
            sems((micro,)),
            sems((micro,)),
            sems((micro,)),
            sems((micro,)),
            sems((micro,)),
            sems((2,)),
            sems((2,)),
        ],
        compiler_params=pltpu.CompilerParams(
            collective_id=0, has_side_effects=True, vmem_limit_bytes=52 * 2**20
        ),
    )(plan.T, order, inputs, cotangent, weights, old_factor)


def solution(mesh):
    return jax.shard_map(
        functools.partial(shards, mesh.shape["section"], mesh.shape["dp"]),
        mesh=mesh,
        in_specs=(
            P(None, "dp", None),
            P(None, "dp", None),
            P("section", "dp", None),
            P("section", None, "dp", None),
            P(),
            P(),
        ),
        out_specs=(
            P("section", None, "dp", None),
            P("section", None, "dp", None),
            P("section", "dp", None),
        ),
        check_vma=False,
    )
```

```python
import functools

import jax
import jax.numpy as jnp
from jax import lax
from jax.experimental import pallas as pl
from jax.experimental.pallas import tpu as pltpu
from jax.sharding import PartitionSpec as P

RETAIN = 0.6
DAMPING = 0.1
TERMS = 8
CORES = 2
BAND = 16
MESH = pl.DeviceIdType.MESH


def kernel(
    sections,
    replicas,
    pieces,
    plan_ref,
    order_ref,
    x_ref,
    ct_ref,
    w_ref,
    old_ref,
    out_ref,
    grad_ref,
    inv_ref,
    w,
    wt,
    ends,
    x_in,
    g_in,
    out,
    grad,
    slope,
    delta,
    feats,
    old_own,
    old_all,
    matrix,
    lent,
    local_sem,
    store_sem,
    ring_send,
    ring_recv,
    sib_sem,
    lend_sem,
    relay_send,
    relay_recv,
    back_send,
    back_recv,
    fwd_send,
    fwd_recv,
    bwd_send,
    bwd_recv,
    feat_send,
    feat_recv,
    feat_pass,
    feat_got,
    old_sem,
    old_pass,
):
    micro, rows, width = x_in.shape
    shard = w_ref.shape[1]
    band, order_size = old_ref.shape[2], old_ref.shape[3]
    piece = width // pieces
    unit = piece // 2
    sizes = [3 * unit] + [piece] * (pieces - 2) + [unit]
    cuts = [pl.ds(sum(sizes[:j]), sizes[j]) for j in range(pieces)]
    zs = replicas // CORES
    lent_rows = lent.shape[1]
    bands = lent_rows // BAND
    parts = (
        (0, shard - 2 * lent_rows),
        (shard - 2 * lent_rows, lent_rows),
        (shard - lent_rows, lent_rows),
    )
    group = max(1, sections // 4)
    s = lax.axis_index("section")
    r = lax.axis_index("dp")
    z, core = r // CORES, r % CORES
    first, last = s == 0, s == sections - 1
    borrows, lends = s < group, s >= sections - group
    partner = (s + sections - group) % sections
    partner = jnp.where(borrows, partner, jnp.where(lends, s - (sections - group), s))
    sibling = z * CORES + (1 - core)
    up, down = jnp.minimum(s + 1, sections - 1), jnp.maximum(s - 1, 0)

    def along_z(steps):
        return (z + steps) % zs

    def copy(src, dst, send, recv, **device):
        return pltpu.make_async_remote_copy(
            src_ref=src,
            dst_ref=dst,
            send_sem=send,
            recv_sem=recv,
            device_id=device,
            device_id_type=MESH,
        )

    own_w = pltpu.make_async_copy(
        w_ref.at[0], w.at[pl.ds(pl.multiple_of(r * shard, 16), shard)], local_sem.at[0]
    )
    own_w.start()
    load_old = pltpu.make_async_copy(old_ref.at[0], old_own, local_sem.at[1])
    load_old.start()
    load_x = pltpu.make_async_copy(x_ref, ends, local_sem.at[2])
    load_ct = pltpu.make_async_copy(ct_ref, ends, local_sem.at[2])

    @pl.when(first)
    def _():
        load_x.start()

    @pl.when(last)
    def _():
        load_ct.start()

    barrier = pltpu.get_barrier_semaphore()

    def greet(i, _):
        there = along_z(i) * CORES + core
        pl.semaphore_signal(barrier, inc=1, device_id={"dp": there}, device_id_type=MESH)
        return 0

    lax.fori_loop(1, zs, greet, 0)
    pl.semaphore_signal(barrier, inc=1, device_id={"dp": sibling}, device_id_type=MESH)
    helped = jnp.logical_or(borrows, lends)

    @pl.when(jnp.logical_not(last))
    def _():
        pl.semaphore_signal(barrier, inc=1, device_id={"section": up}, device_id_type=MESH)

    @pl.when(jnp.logical_not(first))
    def _():
        pl.semaphore_signal(barrier, inc=1, device_id={"section": down}, device_id_type=MESH)

    @pl.when(helped)
    def _():
        pl.semaphore_signal(barrier, inc=1, device_id={"section": partner}, device_id_type=MESH)

    peers = zs + jnp.where(first, 0, 1) + jnp.where(last, 0, 1) + jnp.where(helped, 1, 0)
    pl.semaphore_wait(barrier, peers)

    def w_rows(at_z, part):
        start = (at_z * CORES + core) * shard + parts[part][0]
        return w.at[pl.ds(pl.multiple_of(start, 16), parts[part][1])]

    def own_rows(part):
        return w_ref.at[0, pl.ds(*parts[part])]

    def to_sibling(rows_there):
        copy(rows_there, rows_there, sib_sem.at[0], sib_sem.at[1], dp=sibling).start()

    def next_z(way):
        return along_z(1 if way == 0 else zs - 1) * CORES + core

    def from_z(way, hop):
        return along_z(zs - hop if way == 0 else hop)

    def hops(way, part):
        return zs // 2 if (way == 0) == (part == 0) else zs // 2 - 1

    def ring_copy(way, hop, part):
        spot = hop * 3 + part
        dst = w_rows(from_z(way, hop), part)
        src = own_rows(part) if hop == 0 else dst
        return copy(src, dst, ring_send.at[way, spot], ring_recv.at[way, spot], dp=next_z(way))

    def ring_arrival(way, hop, part):
        spot = hop * 3 + part
        here = w_rows(from_z(way, hop + 1), part)
        copy(
            here, here, ring_send.at[way, spot], ring_recv.at[way, spot], dp=next_z(way)
        ).wait_recv()
        return here

    def lent_band(at_z, i):
        return lent.at[at_z, pl.ds(i * BAND, BAND)]

    def lend(i):
        start = parts[2][0] + i * BAND
        return copy(
            w_ref.at[0, pl.ds(start, BAND)],
            lent_band(z, i),
            lend_sem.at[0, i],
            lend_sem.at[1, i],
            section=partner,
        )

    def relay_copy(way, hop, i, at=0):
        here = lent_band(from_z(way, hop + at), i)
        return copy(
            here, here, relay_send.at[way, hop, i], relay_recv.at[way, hop, i], dp=next_z(way)
        )

    def give_back(way, hop, i):
        at_z = from_z(way, hop + 1)
        start = (at_z * CORES + core) * shard + parts[2][0] + i * BAND
        return copy(
            lent_band(at_z, i),
            w.at[pl.ds(pl.multiple_of(start, 16), BAND)],
            back_send.at[way, hop, i],
            back_recv.at[way, hop, i],
            section=partner,
        )

    def back_arrival(way, hop):
        for i in range(bands):
            give_back(way, hop, i).wait_recv()
        to_sibling(w_rows(from_z(way, hop + 1), 2))

    lent_hops = (zs // 2, zs // 2 - 1)

    def ring(some_parts, extra):
        for hop in range(zs // 2 + 1):
            for part in some_parts:
                for way in range(2):
                    came = None
                    if 0 < hop <= hops(way, part):
                        came = ring_arrival(way, hop - 1, part)
                    if hop < hops(way, part):
                        ring_copy(way, hop, part).start()
                    if came is not None:
                        to_sibling(came)
            if hop == 0:
                own_w.wait()
                to_sibling(w.at[pl.ds(pl.multiple_of(r * shard, 16), shard)])
            if hop >= 2:
                extra(hop - 2)
        extra(zs // 2 - 1)

    @pl.when(borrows)
    def _():
        for i in range(bands):
            lend(i).start()

        def extra(hop):
            for way in range(2):
                if hop < lent_hops[way]:
                    back_arrival(way, hop)

        ring((0, 1), extra)

    @pl.when(lends)
    def _():
        for hop in range(zs // 2 + 1):
            for i in range(bands):
                if hop == 0:
                    lend(i).wait_recv()
                for way in range(2):
                    came = 0 < hop <= lent_hops[way]
                    if came:
                        relay_copy(way, hop - 1, i, 1).wait_recv()
                    if hop < lent_hops[way]:
                        relay_copy(way, hop, i).start()
                    if came:
                        give_back(way, hop - 1, i).start()

    @pl.when(jnp.logical_not(borrows))
    def _():
        ring((0, 1, 2), lambda hop: None)

    load_old.wait()
    block = plan_ref[0, s]
    filled = plan_ref[2, s]
    old_all[z, core] = old_own[block]

    def send_old(i, _):
        here = old_all.at[z, core]
        copy(here, here, old_sem.at[0], old_sem.at[1], dp=along_z(i) * CORES + core).start()
        return 0

    lax.fori_loop(1, zs, send_old, 0)
    all_sib = w.at[pl.ds(0, zs * shard)]
    sib_wait = copy(all_sib, all_sib, sib_sem.at[0], sib_sem.at[1], dp=sibling)
    sib_wait.wait_recv()

    def turn_weights():
        tile = 2 * 128
        spots = lax.broadcasted_iota(jnp.int32, (tile, tile), 0)
        eye = (spots == lax.broadcasted_iota(jnp.int32, (tile, tile), 1)).astype(jnp.bfloat16)

        def turn(i, _):
            at = pl.ds(pl.multiple_of(i * tile, tile), tile)
            for j in range(pieces):
                cols = pl.ds(j * piece, piece)
                wt[cols, at] = lax.dot_general(
                    w[at, cols], eye, (((0,), (0,)), ((), ())), preferred_element_type=jnp.float32
                ).astype(jnp.bfloat16)
            return 0

        lax.fori_loop(0, width // tile, turn, 0)

    def store(ref, c, whole_ref, sem):
        return pltpu.make_async_copy(ref.at[c], whole_ref.at[0, c], sem)

    def by_pieces(value, matrix_ref, finish):
        before = None
        for j, cols in enumerate(cuts):
            product = jnp.dot(value, matrix_ref[:, cols], preferred_element_type=jnp.float32)
            if before is not None:
                finish(*before)
            before = (j, cols, product)
        finish(*before)

    def forward(c, count, sends):
        for i in range(count):
            arrival = copy(
                x_in.at[c + i], x_in.at[c + i], fwd_send.at[c + i], fwd_recv.at[c + i], section=up
            )
            if sends:

                @pl.when(first)
                def _():
                    x_in[c + i] = ends[order_ref[c + i]]

                @pl.when(jnp.logical_not(first))
                def _():
                    arrival.wait_recv()

            else:
                arrival.wait_recv()

        these = pl.ds(c, count)
        x = x_in[these].reshape(count * rows, width)

        def finish(_, cols, pre):
            pre = pre.reshape(count, rows, cols.size)
            gate = jax.nn.sigmoid(pre)
            out[these, :, cols] = (x_in[these, :, cols].astype(jnp.float32) + pre * gate).astype(
                jnp.bfloat16
            )
            if sends:
                copy(
                    out.at[c, :, cols],
                    x_in.at[c, :, cols],
                    fwd_send.at[c],
                    fwd_recv.at[c],
                    section=up,
                ).start()
            slope[these, :, cols] = gate * (1.0 + pre * (1.0 - gate))

        by_pieces(x, w, finish)
        for i in range(count):
            store(out, c + i, out_ref, store_sem.at[0, c + i]).start()

    def forward_step(c, _):
        forward(c, 1, True)
        return 0

    @pl.when(first)
    def _():
        load_x.wait()

    @pl.when(s >= sections // 2)
    def _():
        turn_weights()

    @pl.when(jnp.logical_not(last))
    def _():
        lax.fori_loop(0, micro, forward_step, 0)

    @pl.when(s < sections // 2)
    def _():
        turn_weights()

    own_old = old_all.at[:, core]
    some_old = old_all.at[pl.ds(0, zs - 1), core]
    copy(some_old, some_old, old_sem.at[0], old_sem.at[1], dp=sibling).wait_recv()
    pass_old = copy(own_old, own_old, old_pass.at[0], old_pass.at[1], dp=sibling)
    pass_old.start()
    pass_old.wait_recv()
    scale = (1.0 - RETAIN) / (filled * (rows * replicas)).astype(jnp.float32)
    spots = lax.broadcasted_iota(jnp.int32, (order_size, order_size), 0)
    eye = spots == lax.broadcasted_iota(jnp.int32, (order_size, order_size), 1)
    matrix[...] = RETAIN * old_all[...].reshape(order_size, order_size) + jnp.where(
        eye, DAMPING, 0.0
    )
    place = block % (width // order_size)
    from_input = block < width // order_size

    def gradient_in(c):
        @pl.when(last)
        def _():
            g_in[c] = ends[order_ref[c]]

        @pl.when(jnp.logical_not(last))
        def _():
            copy(g_in.at[c], g_in.at[c], bwd_send.at[c], bwd_recv.at[c], section=down).wait_recv()

        delta[c] = (g_in[c].astype(jnp.float32) * slope[c]).astype(jnp.bfloat16)

    def choose_features(c):
        chosen = jnp.zeros((rows, order_size), jnp.bfloat16)
        for j in range(width // order_size):
            cols = pl.ds(j * order_size, order_size)
            here = jnp.where(from_input, x_in[c, :, cols], delta[c, :, cols])
            chosen = jnp.where(place == j, here, chosen)
        feats[c, core, z] = jnp.where(c < filled, chosen, jnp.zeros_like(chosen))


    def feature_copies(c):
        copies = []
        for i in sorted(range(1, zs), key=lambda i: -min(i, zs - i)):
            here = feats.at[c, core, z]
            there = along_z(i) * CORES + core
            copies.append(copy(here, here, feat_send.at[c], feat_recv.at[c], dp=there))
        return copies

    def share_features(c):
        for each in feature_copies(c):
            each.start()

    def feats_in(c):
        some = feats.at[c, core, pl.ds(0, zs - 1)]
        return copy(some, some, feat_send.at[c], feat_recv.at[c], dp=sibling)

    def feats_pass(c):
        here = feats.at[c, core]
        return copy(here, here, feat_pass.at[c], feat_got.at[c], dp=sibling)

    def pass_features(c, _=0):
        feats_in(c).wait_recv()
        feats_pass(c).start()
        return 0

    def add_stats(c, _=0):
        feats_pass(c).wait_recv()
        v = feats[c].reshape(replicas * rows, order_size)
        matrix[...] += scale * lax.dot_general(
            v, v, (((0,), (0,)), ((), ())), preferred_element_type=jnp.float32
        )
        return 0

    def backward(c, count, chosen_before):
        leaving = [each for b in chosen_before for each in feature_copies(b)]
        for i in range(count):
            gradient_in(c + i)
        these = pl.ds(c, count)
        d = delta[these].reshape(count * rows, width)

        def finish(j, cols, back):
            back = back.reshape(count, rows, cols.size)
            grad[these, :, cols] = (g_in[these, :, cols].astype(jnp.float32) + back).astype(
                jnp.bfloat16
            )
            copy(
                grad.at[c, :, cols],
                g_in.at[c, :, cols],
                bwd_send.at[c],
                bwd_recv.at[c],
                section=down,
            ).start()
            for each in leaving[j::pieces]:
                each.start()

        by_pieces(d, wt, finish)
        for i in range(1, count):
            copy(
                grad.at[c + i], g_in.at[c + i], bwd_send.at[c + i], bwd_recv.at[c + i], section=down
            ).start()
        for i in range(count):
            choose_features(c + i)
            store(grad, c + i, grad_ref, store_sem.at[1, c + i]).start()

    def backward_step(c, _):
        backward(c, 1, [c - 1])
        return 0

    near_last = jnp.logical_and(s >= sections - 2, jnp.logical_not(first))

    @pl.when(jnp.logical_not(jnp.logical_or(first, near_last)))
    def _():
        backward(0, 1, [])
        lax.fori_loop(1, micro, backward_step, 0)
        share_features(micro - 1)

    @pl.when(near_last)
    def _():
        @pl.when(last)
        def _():
            load_ct.wait()

        def turn_round(c, count, chosen_before):
            @pl.when(last)
            def _():
                forward(c, count, False)

            backward(c, count, chosen_before)

        def by_twos(i, _):
            turn_round(1 + 2 * i, 2, [2 * i - 1, 2 * i])
            return 0

        turn_round(0, 1, [])
        turn_round(1, 2, [0])
        lax.fori_loop(1, (micro - 2) // 2, by_twos, 0)
        turn_round(micro - 1, 1, [micro - 3, micro - 2])
        share_features(micro - 1)

    @pl.when(jnp.logical_not(first))
    def _():
        lax.fori_loop(0, micro, pass_features, 0)
        lax.fori_loop(0, micro, add_stats, 0)

    lag = min(3, micro - 1)

    def backward_first(c, _):
        gradient_in(c)
        choose_features(c)
        share_features(c)

        @pl.when(c >= lag)
        def _():
            pass_features(c - lag)

        @pl.when(c > lag)
        def _():
            add_stats(c - lag - 1)

        return 0

    @pl.when(first)
    def _():
        lax.fori_loop(0, micro, backward_first, 0)
        lax.fori_loop(micro - lag, micro - 1, pass_features, 0)
        add_stats(micro - lag - 1)

        def all_gradients(j, _):
            cols = pl.ds(pl.multiple_of(j * piece, 128), piece)
            d = delta[...].reshape(micro * rows, width)
            back = jnp.dot(d, wt[:, cols], preferred_element_type=jnp.float32)
            total = g_in[:, :, cols].astype(jnp.float32) + back.reshape(micro, rows, piece)
            grad[:, :, cols] = total.astype(jnp.bfloat16)
            return 0

        lax.fori_loop(0, pieces, all_gradients, 0)

        def store_all(c, _):
            store(grad, c, grad_ref, store_sem.at[1, c]).start()
            return 0

        lax.fori_loop(0, micro, store_all, 0)
        lax.fori_loop(micro - lag, micro - 1, add_stats, 0)
        pass_features(micro - 1)
        add_stats(micro - 1)

    full = matrix[...]
    bound = jnp.max(jnp.sum(jnp.abs(full), axis=1, keepdims=True), axis=0, keepdims=True)
    inverse_bound = 1.0 / bound
    factor = (full * inverse_bound).astype(jnp.bfloat16)
    row_ids = lax.broadcasted_iota(jnp.int32, (band, order_size), 0) + r * band
    ones = (row_ids == lax.broadcasted_iota(jnp.int32, (band, order_size), 1)).astype(jnp.float32)
    total = 2.0 * ones - matrix[pl.ds(pl.multiple_of(r * band, 8), band), :] * inverse_bound
    for _ in range(TERMS - 2):
        product = jnp.dot(
            total.astype(jnp.bfloat16), factor, preferred_element_type=jnp.float32
        )
        total = ones + total - product
    inv_ref[0] = total * inverse_bound

    def drain_ring(some_parts):
        for part in some_parts:
            for way in range(2):
                for hop in range(hops(way, part)):
                    ring_copy(way, hop, part).wait_send()

    drain_ring((0, 1))

    @pl.when(borrows)
    def _():
        for i in range(bands):
            lend(i).wait_send()

    @pl.when(jnp.logical_not(borrows))
    def _():
        drain_ring((2,))

    @pl.when(lends)
    def _():
        for way in range(2):
            for hop in range(lent_hops[way]):
                for i in range(bands):
                    relay_copy(way, hop, i).wait_send()
                    give_back(way, hop, i).wait_send()

    sib_wait.wait_send()
    copy(some_old, some_old, old_sem.at[0], old_sem.at[1], dp=sibling).wait_send()
    pass_old.wait_send()

    def drain(c, _):
        feats_in(c).wait_send()
        feats_pass(c).wait_send()
        store(out, c, out_ref, store_sem.at[0, c]).wait()
        store(grad, c, grad_ref, store_sem.at[1, c]).wait()

        @pl.when(jnp.logical_not(last))
        def _():
            copy(out.at[c], x_in.at[c], fwd_send.at[c], fwd_recv.at[c], section=up).wait_send()

        @pl.when(jnp.logical_not(first))
        def _():
            copy(grad.at[c], g_in.at[c], bwd_send.at[c], bwd_recv.at[c], section=down).wait_send()

        return 0

    lax.fori_loop(0, micro, drain, 0)


def shards(sections, replicas, inputs, cotangent, weights, old_factor, plan, order):
    micro, rows, width = inputs.shape
    _, blocks, band, order_size = old_factor.shape
    shard = weights.shape[1]
    lent_rows = shard // 16 * 3 // 10 * 16
    pieces = 5 if width % 640 == 0 else width // 128
    vmem = pl.BlockSpec(memory_space=pltpu.VMEM)
    smem = pl.BlockSpec(memory_space=pltpu.SMEM)
    free = pl.BlockSpec(memory_space=pl.ANY)
    hbm = pl.BlockSpec(memory_space=pltpu.HBM)
    sems = pltpu.SemaphoreType.DMA
    zs = replicas // CORES
    acts = pltpu.VMEM((micro, rows, width), jnp.bfloat16)
    return pl.pallas_call(
        functools.partial(kernel, sections, replicas, pieces),
        out_shape=(
            jax.ShapeDtypeStruct((1, micro, rows, width), jnp.bfloat16),
            jax.ShapeDtypeStruct((1, micro, rows, width), jnp.bfloat16),
            jax.ShapeDtypeStruct((1, band, order_size), jnp.float32),
        ),
        in_specs=[smem, smem, hbm, hbm, hbm, hbm],
        out_specs=(free, free, vmem),
        scratch_shapes=[
            pltpu.VMEM((width, width), jnp.bfloat16),
            pltpu.VMEM((width, width), jnp.bfloat16),
            acts,
            acts,
            acts,
            acts,
            acts,
            pltpu.VMEM((micro, rows, width), jnp.float32),
            acts,
            pltpu.VMEM((micro, CORES, zs, rows, order_size), jnp.bfloat16),
            pltpu.VMEM((blocks, band, order_size), jnp.float32),
            pltpu.VMEM((zs, CORES, band, order_size), jnp.float32),
            pltpu.VMEM((order_size, order_size), jnp.float32),
            pltpu.VMEM((zs, lent_rows, width), jnp.bfloat16),
            sems((3,)),
            sems((2, micro)),
            sems((2, 3 * (zs // 2))),
            sems((2, 3 * (zs // 2))),
            sems((2,)),
            sems((2, lent_rows // BAND)),
            sems((2, zs // 2, lent_rows // BAND)),
            sems((2, zs // 2, lent_rows // BAND)),
            sems((2, zs // 2, lent_rows // BAND)),
            sems((2, zs // 2, lent_rows // BAND)),
            sems((micro,)),
            sems((micro,)),
            sems((micro,)),
            sems((micro,)),
            sems((micro,)),
            sems((micro,)),
            sems((micro,)),
            sems((micro,)),
            sems((2,)),
            sems((2,)),
        ],
        compiler_params=pltpu.CompilerParams(
            collective_id=0, has_side_effects=True, vmem_limit_bytes=52 * 2**20
        ),
    )(plan.T, order, inputs, cotangent, weights, old_factor)


def solution(mesh):
    return jax.shard_map(
        functools.partial(shards, mesh.shape["section"], mesh.shape["dp"]),
        mesh=mesh,
        in_specs=(
            P(None, "dp", None),
            P(None, "dp", None),
            P("section", "dp", None),
            P("section", None, "dp", None),
            P(),
            P(),
        ),
        out_specs=(
            P("section", None, "dp", None),
            P("section", None, "dp", None),
            P("section", "dp", None),
        ),
        check_vma=False,
    )
```

```python
import functools

import jax
import jax.numpy as jnp
from jax import lax
from jax.experimental import pallas as pl
from jax.experimental.pallas import tpu as pltpu
from jax.sharding import PartitionSpec as P

RETAIN = 0.6
DAMPING = 0.1
TERMS = 8
CORES = 2
BAND = 16
MESH = pl.DeviceIdType.MESH


def kernel(
    sections,
    replicas,
    pieces,
    plan_ref,
    order_ref,
    x_ref,
    ct_ref,
    w_ref,
    old_ref,
    out_ref,
    grad_ref,
    inv_ref,
    w,
    wt,
    ends,
    x_in,
    g_in,
    out,
    grad,
    slope,
    delta,
    feats,
    old_own,
    old_all,
    matrix,
    lent,
    local_sem,
    store_sem,
    ring_send,
    ring_recv,
    sib_sem,
    lend_sem,
    relay_send,
    relay_recv,
    back_send,
    back_recv,
    fwd_send,
    fwd_recv,
    bwd_send,
    bwd_recv,
    feat_send,
    feat_recv,
    feat_pass,
    feat_got,
    old_sem,
    old_pass,
):
    micro, rows, width = x_in.shape
    shard = w_ref.shape[1]
    band, order_size = old_ref.shape[2], old_ref.shape[3]
    piece = width // pieces
    zs = replicas // CORES
    lent_rows = lent.shape[1]
    bands = lent_rows // BAND
    parts = (
        (0, shard - 2 * lent_rows),
        (shard - 2 * lent_rows, lent_rows),
        (shard - lent_rows, lent_rows),
    )
    group = max(1, sections // 4)
    s = lax.axis_index("section")
    r = lax.axis_index("dp")
    z, core = r // CORES, r % CORES
    first, last = s == 0, s == sections - 1
    borrows, lends = s < group, s >= sections - group
    partner = (s + sections - group) % sections
    partner = jnp.where(borrows, partner, jnp.where(lends, s - (sections - group), s))
    sibling = z * CORES + (1 - core)
    up, down = jnp.minimum(s + 1, sections - 1), jnp.maximum(s - 1, 0)

    def along_z(steps):
        return (z + steps) % zs

    def copy(src, dst, send, recv, **device):
        return pltpu.make_async_remote_copy(
            src_ref=src,
            dst_ref=dst,
            send_sem=send,
            recv_sem=recv,
            device_id=device,
            device_id_type=MESH,
        )

    own_w = pltpu.make_async_copy(
        w_ref.at[0], w.at[pl.ds(pl.multiple_of(r * shard, 16), shard)], local_sem.at[0]
    )
    own_w.start()
    load_old = pltpu.make_async_copy(old_ref.at[0], old_own, local_sem.at[1])
    load_old.start()
    load_x = pltpu.make_async_copy(x_ref, ends, local_sem.at[2])
    load_ct = pltpu.make_async_copy(ct_ref, ends, local_sem.at[2])

    @pl.when(first)
    def _():
        load_x.start()

    @pl.when(last)
    def _():
        load_ct.start()

    barrier = pltpu.get_barrier_semaphore()

    def greet(i, _):
        there = along_z(i) * CORES + core
        pl.semaphore_signal(barrier, inc=1, device_id={"dp": there}, device_id_type=MESH)
        return 0

    lax.fori_loop(1, zs, greet, 0)
    pl.semaphore_signal(barrier, inc=1, device_id={"dp": sibling}, device_id_type=MESH)
    helped = jnp.logical_or(borrows, lends)

    @pl.when(jnp.logical_not(last))
    def _():
        pl.semaphore_signal(barrier, inc=1, device_id={"section": up}, device_id_type=MESH)

    @pl.when(jnp.logical_not(first))
    def _():
        pl.semaphore_signal(barrier, inc=1, device_id={"section": down}, device_id_type=MESH)

    @pl.when(helped)
    def _():
        pl.semaphore_signal(barrier, inc=1, device_id={"section": partner}, device_id_type=MESH)

    peers = zs + jnp.where(first, 0, 1) + jnp.where(last, 0, 1) + jnp.where(helped, 1, 0)
    pl.semaphore_wait(barrier, peers)

    def w_rows(at_z, part):
        start = (at_z * CORES + core) * shard + parts[part][0]
        return w.at[pl.ds(pl.multiple_of(start, 16), parts[part][1])]

    def own_rows(part):
        return w_ref.at[0, pl.ds(*parts[part])]

    def to_sibling(rows_there):
        copy(rows_there, rows_there, sib_sem.at[0], sib_sem.at[1], dp=sibling).start()

    def next_z(way):
        return along_z(1 if way == 0 else zs - 1) * CORES + core

    def from_z(way, hop):
        return along_z(zs - hop if way == 0 else hop)

    def hops(way, part):
        return zs // 2 if (way == 0) == (part == 0) else zs // 2 - 1

    def ring_copy(way, hop, part):
        spot = hop * 3 + part
        dst = w_rows(from_z(way, hop), part)
        src = own_rows(part) if hop == 0 else dst
        return copy(src, dst, ring_send.at[way, spot], ring_recv.at[way, spot], dp=next_z(way))

    def ring_arrival(way, hop, part):
        spot = hop * 3 + part
        here = w_rows(from_z(way, hop + 1), part)
        copy(
            here, here, ring_send.at[way, spot], ring_recv.at[way, spot], dp=next_z(way)
        ).wait_recv()
        return here

    def lent_band(at_z, i):
        return lent.at[at_z, pl.ds(i * BAND, BAND)]

    def lend(i):
        start = parts[2][0] + i * BAND
        return copy(
            w_ref.at[0, pl.ds(start, BAND)],
            lent_band(z, i),
            lend_sem.at[0, i],
            lend_sem.at[1, i],
            section=partner,
        )

    def relay_copy(way, hop, i, at=0):
        here = lent_band(from_z(way, hop + at), i)
        return copy(
            here, here, relay_send.at[way, hop, i], relay_recv.at[way, hop, i], dp=next_z(way)
        )

    def give_back(way, hop, i):
        at_z = from_z(way, hop + 1)
        start = (at_z * CORES + core) * shard + parts[2][0] + i * BAND
        return copy(
            lent_band(at_z, i),
            w.at[pl.ds(pl.multiple_of(start, 16), BAND)],
            back_send.at[way, hop, i],
            back_recv.at[way, hop, i],
            section=partner,
        )

    def back_arrival(way, hop):
        for i in range(bands):
            give_back(way, hop, i).wait_recv()
        to_sibling(w_rows(from_z(way, hop + 1), 2))

    lent_hops = (zs // 2, zs // 2 - 1)

    def ring(some_parts, extra):
        for hop in range(zs // 2 + 1):
            for part in some_parts:
                for way in range(2):
                    came = None
                    if 0 < hop <= hops(way, part):
                        came = ring_arrival(way, hop - 1, part)
                    if hop < hops(way, part):
                        ring_copy(way, hop, part).start()
                    if came is not None:
                        to_sibling(came)
            if hop == 0:
                own_w.wait()
                to_sibling(w.at[pl.ds(pl.multiple_of(r * shard, 16), shard)])
            if hop >= 2:
                extra(hop - 2)
        extra(zs // 2 - 1)

    @pl.when(borrows)
    def _():
        for i in range(bands):
            lend(i).start()

        def extra(hop):
            for way in range(2):
                if hop < lent_hops[way]:
                    back_arrival(way, hop)

        ring((0, 1), extra)

    @pl.when(lends)
    def _():
        for hop in range(zs // 2 + 1):
            for i in range(bands):
                if hop == 0:
                    lend(i).wait_recv()
                for way in range(2):
                    came = 0 < hop <= lent_hops[way]
                    if came:
                        relay_copy(way, hop - 1, i, 1).wait_recv()
                    if hop < lent_hops[way]:
                        relay_copy(way, hop, i).start()
                    if came:
                        give_back(way, hop - 1, i).start()

    @pl.when(jnp.logical_not(borrows))
    def _():
        ring((0, 1, 2), lambda hop: None)

    load_old.wait()
    block = plan_ref[0, s]
    filled = plan_ref[2, s]
    old_all[z, core] = old_own[block]

    def send_old(i, _):
        here = old_all.at[z, core]
        copy(here, here, old_sem.at[0], old_sem.at[1], dp=along_z(i) * CORES + core).start()
        return 0

    lax.fori_loop(1, zs, send_old, 0)
    all_sib = w.at[pl.ds(0, zs * shard)]
    sib_wait = copy(all_sib, all_sib, sib_sem.at[0], sib_sem.at[1], dp=sibling)
    sib_wait.wait_recv()

    def turn_weights():
        tile = 2 * 128
        spots = lax.broadcasted_iota(jnp.int32, (tile, tile), 0)
        eye = (spots == lax.broadcasted_iota(jnp.int32, (tile, tile), 1)).astype(jnp.bfloat16)

        def turn(i, _):
            at = pl.ds(pl.multiple_of(i * tile, tile), tile)
            for j in range(pieces):
                cols = pl.ds(j * piece, piece)
                wt[cols, at] = lax.dot_general(
                    w[at, cols], eye, (((0,), (0,)), ((), ())), preferred_element_type=jnp.float32
                ).astype(jnp.bfloat16)
            return 0

        lax.fori_loop(0, width // tile, turn, 0)

    def store(ref, c, whole_ref, sem):
        return pltpu.make_async_copy(ref.at[c], whole_ref.at[0, c], sem)

    def by_pieces(value, matrix_ref, finish):
        before = None
        for j in range(pieces):
            cols = pl.ds(j * piece, piece)
            product = jnp.dot(value, matrix_ref[:, cols], preferred_element_type=jnp.float32)
            if before is not None:
                finish(*before)
            before = (cols, product)
        finish(*before)

    def forward(c, count, sends):
        for i in range(count):
            arrival = copy(
                x_in.at[c + i], x_in.at[c + i], fwd_send.at[c + i], fwd_recv.at[c + i], section=up
            )
            if sends:

                @pl.when(first)
                def _():
                    x_in[c + i] = ends[order_ref[c + i]]

                @pl.when(jnp.logical_not(first))
                def _():
                    arrival.wait_recv()

            else:
                arrival.wait_recv()

        these = pl.ds(c, count)
        x = x_in[these].reshape(count * rows, width)

        def finish(cols, pre):
            pre = pre.reshape(count, rows, piece)
            gate = jax.nn.sigmoid(pre)
            out[these, :, cols] = (x_in[these, :, cols].astype(jnp.float32) + pre * gate).astype(
                jnp.bfloat16
            )
            if sends:
                copy(
                    out.at[c, :, cols],
                    x_in.at[c, :, cols],
                    fwd_send.at[c],
                    fwd_recv.at[c],
                    section=up,
                ).start()
            slope[these, :, cols] = gate * (1.0 + pre * (1.0 - gate))

        by_pieces(x, w, finish)
        for i in range(count):
            store(out, c + i, out_ref, store_sem.at[0, c + i]).start()

    def forward_step(c, _):
        forward(c, 1, True)
        return 0

    @pl.when(first)
    def _():
        load_x.wait()

    @pl.when(s >= sections // 2)
    def _():
        turn_weights()

    @pl.when(jnp.logical_not(last))
    def _():
        lax.fori_loop(0, micro, forward_step, 0)

    @pl.when(s < sections // 2)
    def _():
        turn_weights()

    own_old = old_all.at[:, core]
    some_old = old_all.at[pl.ds(0, zs - 1), core]
    copy(some_old, some_old, old_sem.at[0], old_sem.at[1], dp=sibling).wait_recv()
    pass_old = copy(own_old, own_old, old_pass.at[0], old_pass.at[1], dp=sibling)
    pass_old.start()
    pass_old.wait_recv()
    scale = (1.0 - RETAIN) / (filled * (rows * replicas)).astype(jnp.float32)
    spots = lax.broadcasted_iota(jnp.int32, (order_size, order_size), 0)
    eye = spots == lax.broadcasted_iota(jnp.int32, (order_size, order_size), 1)
    matrix[...] = RETAIN * old_all[...].reshape(order_size, order_size) + jnp.where(
        eye, DAMPING, 0.0
    )
    place = block % (width // order_size)
    from_input = block < width // order_size

    def gradient_in(c):
        @pl.when(last)
        def _():
            g_in[c] = ends[order_ref[c]]

        @pl.when(jnp.logical_not(last))
        def _():
            copy(g_in.at[c], g_in.at[c], bwd_send.at[c], bwd_recv.at[c], section=down).wait_recv()

        delta[c] = (g_in[c].astype(jnp.float32) * slope[c]).astype(jnp.bfloat16)

    def share_features(c):
        chosen = jnp.zeros((rows, order_size), jnp.bfloat16)
        for j in range(width // order_size):
            cols = pl.ds(j * order_size, order_size)
            here = jnp.where(from_input, x_in[c, :, cols], delta[c, :, cols])
            chosen = jnp.where(place == j, here, chosen)
        feats[c, core, z] = jnp.where(c < filled, chosen, jnp.zeros_like(chosen))

        for i in sorted(range(1, zs), key=lambda i: -min(i, zs - i)):
            here = feats.at[c, core, z]
            there = along_z(i) * CORES + core
            copy(here, here, feat_send.at[c], feat_recv.at[c], dp=there).start()

    def feats_in(c):
        some = feats.at[c, core, pl.ds(0, zs - 1)]
        return copy(some, some, feat_send.at[c], feat_recv.at[c], dp=sibling)

    def feats_pass(c):
        here = feats.at[c, core]
        return copy(here, here, feat_pass.at[c], feat_got.at[c], dp=sibling)

    def pass_features(c, _=0):
        feats_in(c).wait_recv()
        feats_pass(c).start()
        return 0

    def add_stats(c, _=0):
        feats_pass(c).wait_recv()
        v = feats[c].reshape(replicas * rows, order_size)
        matrix[...] += scale * lax.dot_general(
            v, v, (((0,), (0,)), ((), ())), preferred_element_type=jnp.float32
        )
        return 0

    def backward(c, count):
        for i in range(count):
            gradient_in(c + i)
        these = pl.ds(c, count)
        d = delta[these].reshape(count * rows, width)

        def finish(cols, back):
            back = back.reshape(count, rows, piece)
            grad[these, :, cols] = (g_in[these, :, cols].astype(jnp.float32) + back).astype(
                jnp.bfloat16
            )
            copy(
                grad.at[c, :, cols],
                g_in.at[c, :, cols],
                bwd_send.at[c],
                bwd_recv.at[c],
                section=down,
            ).start()

        by_pieces(d, wt, finish)
        for i in range(1, count):
            copy(
                grad.at[c + i], g_in.at[c + i], bwd_send.at[c + i], bwd_recv.at[c + i], section=down
            ).start()
        for i in range(count):
            share_features(c + i)
            store(grad, c + i, grad_ref, store_sem.at[1, c + i]).start()

    def backward_step(c, _):
        backward(c, 1)
        return 0

    near_last = jnp.logical_and(s >= sections - 2, jnp.logical_not(first))

    @pl.when(jnp.logical_not(jnp.logical_or(first, near_last)))
    def _():
        lax.fori_loop(0, micro, backward_step, 0)

    @pl.when(near_last)
    def _():
        @pl.when(last)
        def _():
            load_ct.wait()

        def turn_round(c, count):
            @pl.when(last)
            def _():
                forward(c, count, False)

            backward(c, count)

        def by_twos(i, _):
            turn_round(1 + 2 * i, 2)
            return 0

        turn_round(0, 1)
        lax.fori_loop(0, (micro - 2) // 2, by_twos, 0)
        turn_round(micro - 1, 1)

    @pl.when(jnp.logical_not(first))
    def _():
        lax.fori_loop(0, micro, pass_features, 0)
        lax.fori_loop(0, micro, add_stats, 0)

    lag = min(3, micro - 1)

    def backward_first(c, _):
        gradient_in(c)
        share_features(c)

        @pl.when(c >= lag)
        def _():
            pass_features(c - lag)

        @pl.when(c > lag)
        def _():
            add_stats(c - lag - 1)

        return 0

    @pl.when(first)
    def _():
        lax.fori_loop(0, micro, backward_first, 0)
        lax.fori_loop(micro - lag, micro - 1, pass_features, 0)
        add_stats(micro - lag - 1)

        def all_gradients(j, _):
            cols = pl.ds(pl.multiple_of(j * piece, 128), piece)
            d = delta[...].reshape(micro * rows, width)
            back = jnp.dot(d, wt[:, cols], preferred_element_type=jnp.float32)
            total = g_in[:, :, cols].astype(jnp.float32) + back.reshape(micro, rows, piece)
            grad[:, :, cols] = total.astype(jnp.bfloat16)
            return 0

        lax.fori_loop(0, pieces, all_gradients, 0)

        def store_all(c, _):
            store(grad, c, grad_ref, store_sem.at[1, c]).start()
            return 0

        lax.fori_loop(0, micro, store_all, 0)
        lax.fori_loop(micro - lag, micro - 1, add_stats, 0)
        pass_features(micro - 1)
        add_stats(micro - 1)

    full = matrix[...]
    bound = jnp.max(jnp.sum(jnp.abs(full), axis=1, keepdims=True), axis=0, keepdims=True)
    unit = 1.0 / bound
    factor = (full * unit).astype(jnp.bfloat16)
    row_ids = lax.broadcasted_iota(jnp.int32, (band, order_size), 0) + r * band
    ones = (row_ids == lax.broadcasted_iota(jnp.int32, (band, order_size), 1)).astype(jnp.float32)
    total = 2.0 * ones - matrix[pl.ds(pl.multiple_of(r * band, 8), band), :] * unit
    for _ in range(TERMS - 2):
        product = jnp.dot(
            total.astype(jnp.bfloat16), factor, preferred_element_type=jnp.float32
        )
        total = ones + total - product
    inv_ref[0] = total * unit

    def drain_ring(some_parts):
        for part in some_parts:
            for way in range(2):
                for hop in range(hops(way, part)):
                    ring_copy(way, hop, part).wait_send()

    drain_ring((0, 1))

    @pl.when(borrows)
    def _():
        for i in range(bands):
            lend(i).wait_send()

    @pl.when(jnp.logical_not(borrows))
    def _():
        drain_ring((2,))

    @pl.when(lends)
    def _():
        for way in range(2):
            for hop in range(lent_hops[way]):
                for i in range(bands):
                    relay_copy(way, hop, i).wait_send()
                    give_back(way, hop, i).wait_send()

    sib_wait.wait_send()
    copy(some_old, some_old, old_sem.at[0], old_sem.at[1], dp=sibling).wait_send()
    pass_old.wait_send()

    def drain(c, _):
        feats_in(c).wait_send()
        feats_pass(c).wait_send()
        store(out, c, out_ref, store_sem.at[0, c]).wait()
        store(grad, c, grad_ref, store_sem.at[1, c]).wait()

        @pl.when(jnp.logical_not(last))
        def _():
            copy(out.at[c], x_in.at[c], fwd_send.at[c], fwd_recv.at[c], section=up).wait_send()

        @pl.when(jnp.logical_not(first))
        def _():
            copy(grad.at[c], g_in.at[c], bwd_send.at[c], bwd_recv.at[c], section=down).wait_send()

        return 0

    lax.fori_loop(0, micro, drain, 0)


def shards(sections, replicas, inputs, cotangent, weights, old_factor, plan, order):
    micro, rows, width = inputs.shape
    _, blocks, band, order_size = old_factor.shape
    shard = weights.shape[1]
    lent_rows = shard // 16 * 3 // 10 * 16
    pieces = 5 if width % 640 == 0 else width // 128
    vmem = pl.BlockSpec(memory_space=pltpu.VMEM)
    smem = pl.BlockSpec(memory_space=pltpu.SMEM)
    free = pl.BlockSpec(memory_space=pl.ANY)
    hbm = pl.BlockSpec(memory_space=pltpu.HBM)
    sems = pltpu.SemaphoreType.DMA
    zs = replicas // CORES
    acts = pltpu.VMEM((micro, rows, width), jnp.bfloat16)
    return pl.pallas_call(
        functools.partial(kernel, sections, replicas, pieces),
        out_shape=(
            jax.ShapeDtypeStruct((1, micro, rows, width), jnp.bfloat16),
            jax.ShapeDtypeStruct((1, micro, rows, width), jnp.bfloat16),
            jax.ShapeDtypeStruct((1, band, order_size), jnp.float32),
        ),
        in_specs=[smem, smem, hbm, hbm, hbm, hbm],
        out_specs=(free, free, vmem),
        scratch_shapes=[
            pltpu.VMEM((width, width), jnp.bfloat16),
            pltpu.VMEM((width, width), jnp.bfloat16),
            acts,
            acts,
            acts,
            acts,
            acts,
            pltpu.VMEM((micro, rows, width), jnp.float32),
            acts,
            pltpu.VMEM((micro, CORES, zs, rows, order_size), jnp.bfloat16),
            pltpu.VMEM((blocks, band, order_size), jnp.float32),
            pltpu.VMEM((zs, CORES, band, order_size), jnp.float32),
            pltpu.VMEM((order_size, order_size), jnp.float32),
            pltpu.VMEM((zs, lent_rows, width), jnp.bfloat16),
            sems((3,)),
            sems((2, micro)),
            sems((2, 3 * (zs // 2))),
            sems((2, 3 * (zs // 2))),
            sems((2,)),
            sems((2, lent_rows // BAND)),
            sems((2, zs // 2, lent_rows // BAND)),
            sems((2, zs // 2, lent_rows // BAND)),
            sems((2, zs // 2, lent_rows // BAND)),
            sems((2, zs // 2, lent_rows // BAND)),
            sems((micro,)),
            sems((micro,)),
            sems((micro,)),
            sems((micro,)),
            sems((micro,)),
            sems((micro,)),
            sems((micro,)),
            sems((micro,)),
            sems((2,)),
            sems((2,)),
        ],
        compiler_params=pltpu.CompilerParams(
            collective_id=0, has_side_effects=True, vmem_limit_bytes=52 * 2**20
        ),
    )(plan.T, order, inputs, cotangent, weights, old_factor)


def solution(mesh):
    return jax.shard_map(
        functools.partial(shards, mesh.shape["section"], mesh.shape["dp"]),
        mesh=mesh,
        in_specs=(
            P(None, "dp", None),
            P(None, "dp", None),
            P("section", "dp", None),
            P("section", None, "dp", None),
            P(),
            P(),
        ),
        out_specs=(
            P("section", None, "dp", None),
            P("section", None, "dp", None),
            P("section", "dp", None),
        ),
        check_vma=False,
    )
```

```python
import functools

import jax
import jax.numpy as jnp
from jax import lax
from jax.experimental import pallas as pl
from jax.experimental.pallas import tpu as pltpu
from jax.sharding import PartitionSpec as P

RETAIN = 0.6
DAMPING = 0.1
TERMS = 8
CORES = 2
BAND = 16
MESH = pl.DeviceIdType.MESH


def kernel(
    sections,
    replicas,
    pieces,
    plan_ref,
    order_ref,
    x_ref,
    ct_ref,
    w_ref,
    old_ref,
    out_ref,
    grad_ref,
    inv_ref,
    w,
    wt,
    ends,
    x_in,
    g_in,
    out,
    grad,
    slope,
    delta,
    feats,
    old_own,
    old_all,
    matrix,
    lent,
    local_sem,
    store_sem,
    ring_send,
    ring_recv,
    sib_sem,
    lend_sem,
    relay_send,
    relay_recv,
    back_send,
    back_recv,
    fwd_send,
    fwd_recv,
    bwd_send,
    bwd_recv,
    feat_send,
    feat_recv,
    feat_pass,
    feat_got,
    old_sem,
    old_pass,
):
    micro, rows, width = x_in.shape
    shard = w_ref.shape[1]
    band, order_size = old_ref.shape[2], old_ref.shape[3]
    piece = width // pieces
    zs = replicas // CORES
    lent_rows = lent.shape[1]
    bands = lent_rows // BAND
    parts = (
        (0, shard - 2 * lent_rows),
        (shard - 2 * lent_rows, lent_rows),
        (shard - lent_rows, lent_rows),
    )
    group = max(1, sections // 4)
    s = lax.axis_index("section")
    r = lax.axis_index("dp")
    z, core = r // CORES, r % CORES
    first, last = s == 0, s == sections - 1
    borrows, lends = s < group, s >= sections - group
    partner = (s + sections - group) % sections
    partner = jnp.where(borrows, partner, jnp.where(lends, s - (sections - group), s))
    sibling = z * CORES + (1 - core)
    up, down = jnp.minimum(s + 1, sections - 1), jnp.maximum(s - 1, 0)

    def along_z(steps):
        return (z + steps) % zs

    def copy(src, dst, send, recv, **device):
        return pltpu.make_async_remote_copy(
            src_ref=src,
            dst_ref=dst,
            send_sem=send,
            recv_sem=recv,
            device_id=device,
            device_id_type=MESH,
        )

    own_w = pltpu.make_async_copy(
        w_ref.at[0], w.at[pl.ds(pl.multiple_of(r * shard, 16), shard)], local_sem.at[0]
    )
    own_w.start()
    load_old = pltpu.make_async_copy(old_ref.at[0], old_own, local_sem.at[1])
    load_old.start()
    load_x = pltpu.make_async_copy(x_ref, ends, local_sem.at[2])
    load_ct = pltpu.make_async_copy(ct_ref, ends, local_sem.at[2])

    @pl.when(first)
    def _():
        load_x.start()

    @pl.when(last)
    def _():
        load_ct.start()

    barrier = pltpu.get_barrier_semaphore()

    def greet(i, _):
        there = along_z(i) * CORES + core
        pl.semaphore_signal(barrier, inc=1, device_id={"dp": there}, device_id_type=MESH)
        return 0

    lax.fori_loop(1, zs, greet, 0)
    pl.semaphore_signal(barrier, inc=1, device_id={"dp": sibling}, device_id_type=MESH)
    helped = jnp.logical_or(borrows, lends)

    @pl.when(jnp.logical_not(last))
    def _():
        pl.semaphore_signal(barrier, inc=1, device_id={"section": up}, device_id_type=MESH)

    @pl.when(jnp.logical_not(first))
    def _():
        pl.semaphore_signal(barrier, inc=1, device_id={"section": down}, device_id_type=MESH)

    @pl.when(helped)
    def _():
        pl.semaphore_signal(barrier, inc=1, device_id={"section": partner}, device_id_type=MESH)

    peers = zs + jnp.where(first, 0, 1) + jnp.where(last, 0, 1) + jnp.where(helped, 1, 0)
    pl.semaphore_wait(barrier, peers)

    def w_rows(at_z, part):
        start = (at_z * CORES + core) * shard + parts[part][0]
        return w.at[pl.ds(pl.multiple_of(start, 16), parts[part][1])]

    def own_rows(part):
        return w_ref.at[0, pl.ds(*parts[part])]

    def to_sibling(rows_there):
        copy(rows_there, rows_there, sib_sem.at[0], sib_sem.at[1], dp=sibling).start()

    def next_z(way):
        return along_z(1 if way == 0 else zs - 1) * CORES + core

    def from_z(way, hop):
        return along_z(zs - hop if way == 0 else hop)

    def hops(way, part):
        return zs // 2 if (way == 0) == (part == 0) else zs // 2 - 1

    def ring_copy(way, hop, part):
        spot = hop * 3 + part
        dst = w_rows(from_z(way, hop), part)
        src = own_rows(part) if hop == 0 else dst
        return copy(src, dst, ring_send.at[way, spot], ring_recv.at[way, spot], dp=next_z(way))

    def ring_arrival(way, hop, part):
        spot = hop * 3 + part
        here = w_rows(from_z(way, hop + 1), part)
        copy(
            here, here, ring_send.at[way, spot], ring_recv.at[way, spot], dp=next_z(way)
        ).wait_recv()
        return here

    def lent_band(at_z, i):
        return lent.at[at_z, pl.ds(i * BAND, BAND)]

    def lend(i):
        start = parts[2][0] + i * BAND
        return copy(
            w_ref.at[0, pl.ds(start, BAND)],
            lent_band(z, i),
            lend_sem.at[0, i],
            lend_sem.at[1, i],
            section=partner,
        )

    def relay_copy(way, hop, i, at=0):
        here = lent_band(from_z(way, hop + at), i)
        return copy(
            here, here, relay_send.at[way, hop, i], relay_recv.at[way, hop, i], dp=next_z(way)
        )

    def give_back(way, hop, i):
        at_z = from_z(way, hop + 1)
        start = (at_z * CORES + core) * shard + parts[2][0] + i * BAND
        return copy(
            lent_band(at_z, i),
            w.at[pl.ds(pl.multiple_of(start, 16), BAND)],
            back_send.at[way, hop, i],
            back_recv.at[way, hop, i],
            section=partner,
        )

    def back_arrival(way, hop):
        for i in range(bands):
            give_back(way, hop, i).wait_recv()
        to_sibling(w_rows(from_z(way, hop + 1), 2))

    lent_hops = (zs // 2, zs // 2 - 1)

    def ring(some_parts, extra):
        for hop in range(zs // 2 + 1):
            for part in some_parts:
                for way in range(2):
                    came = None
                    if 0 < hop <= hops(way, part):
                        came = ring_arrival(way, hop - 1, part)
                    if hop < hops(way, part):
                        ring_copy(way, hop, part).start()
                    if came is not None:
                        to_sibling(came)
            if hop == 0:
                own_w.wait()
                to_sibling(w.at[pl.ds(pl.multiple_of(r * shard, 16), shard)])
            if hop >= 2:
                extra(hop - 2)
        extra(zs // 2 - 1)

    @pl.when(borrows)
    def _():
        for i in range(bands):
            lend(i).start()

        def extra(hop):
            for way in range(2):
                if hop < lent_hops[way]:
                    back_arrival(way, hop)

        ring((0, 1), extra)

    @pl.when(lends)
    def _():
        for hop in range(zs // 2 + 1):
            for i in range(bands):
                if hop == 0:
                    lend(i).wait_recv()
                for way in range(2):
                    came = 0 < hop <= lent_hops[way]
                    if came:
                        relay_copy(way, hop - 1, i, 1).wait_recv()
                    if hop < lent_hops[way]:
                        relay_copy(way, hop, i).start()
                    if came:
                        give_back(way, hop - 1, i).start()

    @pl.when(jnp.logical_not(borrows))
    def _():
        ring((0, 1, 2), lambda hop: None)

    load_old.wait()
    block = plan_ref[0, s]
    filled = plan_ref[2, s]
    old_all[z, core] = old_own[block]

    def send_old(i, _):
        here = old_all.at[z, core]
        copy(here, here, old_sem.at[0], old_sem.at[1], dp=along_z(i) * CORES + core).start()
        return 0

    lax.fori_loop(1, zs, send_old, 0)
    all_sib = w.at[pl.ds(0, zs * shard)]
    sib_wait = copy(all_sib, all_sib, sib_sem.at[0], sib_sem.at[1], dp=sibling)
    sib_wait.wait_recv()

    def turn_weights():
        tile = 2 * 128
        spots = lax.broadcasted_iota(jnp.int32, (tile, tile), 0)
        eye = (spots == lax.broadcasted_iota(jnp.int32, (tile, tile), 1)).astype(jnp.bfloat16)

        def turn(i, _):
            at = pl.ds(pl.multiple_of(i * tile, tile), tile)
            for j in range(pieces):
                cols = pl.ds(j * piece, piece)
                wt[cols, at] = lax.dot_general(
                    w[at, cols], eye, (((0,), (0,)), ((), ())), preferred_element_type=jnp.float32
                ).astype(jnp.bfloat16)
            return 0

        lax.fori_loop(0, width // tile, turn, 0)

    def store(ref, c, whole_ref, sem):
        return pltpu.make_async_copy(ref.at[c], whole_ref.at[0, c], sem)

    def by_pieces(value, matrix_ref, finish):
        before = None
        for j in range(pieces):
            cols = pl.ds(j * piece, piece)
            product = jnp.dot(value, matrix_ref[:, cols], preferred_element_type=jnp.float32)
            if before is not None:
                finish(*before)
            before = (cols, product)
        finish(*before)

    def forward(c, count, sends):
        for i in range(count):
            arrival = copy(
                x_in.at[c + i], x_in.at[c + i], fwd_send.at[c + i], fwd_recv.at[c + i], section=up
            )
            if sends:

                @pl.when(first)
                def _():
                    x_in[c + i] = ends[order_ref[c + i]]

                @pl.when(jnp.logical_not(first))
                def _():
                    arrival.wait_recv()

            else:
                arrival.wait_recv()

        these = pl.ds(c, count)
        x = x_in[these].reshape(count * rows, width)

        def finish(cols, pre):
            pre = pre.reshape(count, rows, piece)
            gate = jax.nn.sigmoid(pre)
            out[these, :, cols] = (x_in[these, :, cols].astype(jnp.float32) + pre * gate).astype(
                jnp.bfloat16
            )
            if sends:
                copy(
                    out.at[c, :, cols],
                    x_in.at[c, :, cols],
                    fwd_send.at[c],
                    fwd_recv.at[c],
                    section=up,
                ).start()
            slope[these, :, cols] = gate * (1.0 + pre * (1.0 - gate))

        by_pieces(x, w, finish)
        for i in range(count):
            store(out, c + i, out_ref, store_sem.at[0, c + i]).start()

    def forward_step(c, _):
        forward(c, 1, True)
        return 0

    @pl.when(first)
    def _():
        load_x.wait()

    @pl.when(s >= sections // 2)
    def _():
        turn_weights()

    @pl.when(jnp.logical_not(last))
    def _():
        lax.fori_loop(0, micro, forward_step, 0)

    @pl.when(s < sections // 2)
    def _():
        turn_weights()

    own_old = old_all.at[:, core]
    some_old = old_all.at[pl.ds(0, zs - 1), core]
    copy(some_old, some_old, old_sem.at[0], old_sem.at[1], dp=sibling).wait_recv()
    pass_old = copy(own_old, own_old, old_pass.at[0], old_pass.at[1], dp=sibling)
    pass_old.start()
    pass_old.wait_recv()
    scale = (1.0 - RETAIN) / (filled * (rows * replicas)).astype(jnp.float32)
    spots = lax.broadcasted_iota(jnp.int32, (order_size, order_size), 0)
    eye = spots == lax.broadcasted_iota(jnp.int32, (order_size, order_size), 1)
    matrix[...] = RETAIN * old_all[...].reshape(order_size, order_size) + jnp.where(
        eye, DAMPING, 0.0
    )
    place = block % (width // order_size)
    from_input = block < width // order_size

    def gradient_in(c):
        @pl.when(last)
        def _():
            g_in[c] = ends[order_ref[c]]

        @pl.when(jnp.logical_not(last))
        def _():
            copy(g_in.at[c], g_in.at[c], bwd_send.at[c], bwd_recv.at[c], section=down).wait_recv()

        delta[c] = (g_in[c].astype(jnp.float32) * slope[c]).astype(jnp.bfloat16)

    def choose_features(c):
        chosen = jnp.zeros((rows, order_size), jnp.bfloat16)
        for j in range(width // order_size):
            cols = pl.ds(j * order_size, order_size)
            here = jnp.where(from_input, x_in[c, :, cols], delta[c, :, cols])
            chosen = jnp.where(place == j, here, chosen)
        feats[c, core, z] = jnp.where(c < filled, chosen, jnp.zeros_like(chosen))


    right, left = range(1, zs // 2 + 1), range(1, (zs - 1) // 2 + 1)
    near = [d for d in right if d <= 2] + [-d for d in left if d <= 2]
    far = [d for d in right if d > 2] + [-d for d in left if d > 2]

    def send_feats(c, origin, steps, which):
        here = feats.at[c, core, along_z(zs + origin)]
        there = along_z(zs + steps) * CORES + core
        copy(here, here, feat_send.at[which, c], feat_recv.at[which, c], dp=there).start()

    def feats_in(c, which):
        some = feats.at[c, core, pl.ds(0, len(far) if which else len(near))]
        return copy(some, some, feat_send.at[which, c], feat_recv.at[which, c], dp=sibling)

    def send_on(c):
        feats_in(c, 0).wait_recv()
        for d in far:
            back = -2 if d > 0 else 2
            send_feats(c, back, d + back, 1)

    def share_features(c):
        choose_features(c)
        for d in near:
            send_feats(c, 0, d, 0)

        @pl.when(c == micro - 1)
        def _():
            for d in far:
                send_feats(c, 0, d, 1)

        @pl.when(c >= 2)
        def _():
            send_on(c - 2)

    def feats_pass(c):
        here = feats.at[c, core]
        return copy(here, here, feat_pass.at[c], feat_got.at[c], dp=sibling)

    def pass_features(c, _=0):
        @pl.when(c == micro - 1)
        def _():
            feats_in(c, 0).wait_recv()

        if far:
            feats_in(c, 1).wait_recv()
        feats_pass(c).start()
        return 0

    def add_stats(c, _=0):
        feats_pass(c).wait_recv()
        v = feats[c].reshape(replicas * rows, order_size)
        matrix[...] += scale * lax.dot_general(
            v, v, (((0,), (0,)), ((), ())), preferred_element_type=jnp.float32
        )
        return 0

    def backward(c, count):
        for i in range(count):
            gradient_in(c + i)
        these = pl.ds(c, count)
        d = delta[these].reshape(count * rows, width)

        def finish(cols, back):
            back = back.reshape(count, rows, piece)
            grad[these, :, cols] = (g_in[these, :, cols].astype(jnp.float32) + back).astype(
                jnp.bfloat16
            )
            copy(
                grad.at[c, :, cols],
                g_in.at[c, :, cols],
                bwd_send.at[c],
                bwd_recv.at[c],
                section=down,
            ).start()

        by_pieces(d, wt, finish)
        for i in range(1, count):
            copy(
                grad.at[c + i], g_in.at[c + i], bwd_send.at[c + i], bwd_recv.at[c + i], section=down
            ).start()
        for i in range(count):
            share_features(c + i)
            store(grad, c + i, grad_ref, store_sem.at[1, c + i]).start()

    def backward_step(c, _):
        backward(c, 1)
        return 0

    near_last = jnp.logical_and(s >= sections - 2, jnp.logical_not(first))

    @pl.when(jnp.logical_not(jnp.logical_or(first, near_last)))
    def _():
        lax.fori_loop(0, micro, backward_step, 0)

    @pl.when(near_last)
    def _():
        @pl.when(last)
        def _():
            load_ct.wait()

        def turn_round(c, count):
            @pl.when(last)
            def _():
                forward(c, count, False)

            backward(c, count)

        def by_twos(i, _):
            turn_round(1 + 2 * i, 2)
            return 0

        turn_round(0, 1)
        lax.fori_loop(0, (micro - 2) // 2, by_twos, 0)
        turn_round(micro - 1, 1)

    @pl.when(jnp.logical_not(first))
    def _():
        send_on(micro - 2)
        lax.fori_loop(0, micro, pass_features, 0)
        lax.fori_loop(0, micro, add_stats, 0)

    lag = min(4, micro - 1)

    def backward_first(c, _):
        gradient_in(c)
        share_features(c)

        @pl.when(c >= lag)
        def _():
            pass_features(c - lag)

        @pl.when(c > lag)
        def _():
            add_stats(c - lag - 1)

        return 0

    @pl.when(first)
    def _():
        lax.fori_loop(0, micro, backward_first, 0)
        send_on(micro - 2)

        def all_gradients(j, _):
            cols = pl.ds(pl.multiple_of(j * piece, 128), piece)
            d = delta[...].reshape(micro * rows, width)
            back = jnp.dot(d, wt[:, cols], preferred_element_type=jnp.float32)
            total = g_in[:, :, cols].astype(jnp.float32) + back.reshape(micro, rows, piece)
            grad[:, :, cols] = total.astype(jnp.bfloat16)
            return 0

        lax.fori_loop(0, pieces, all_gradients, 0)

        def store_all(c, _):
            store(grad, c, grad_ref, store_sem.at[1, c]).start()
            return 0

        lax.fori_loop(0, micro, store_all, 0)
        add_stats(micro - lag - 1)
        lax.fori_loop(micro - lag, micro - 2, pass_features, 0)
        lax.fori_loop(micro - lag, micro - 2, add_stats, 0)
        pass_features(micro - 2)
        pass_features(micro - 1)
        add_stats(micro - 2)
        add_stats(micro - 1)

    full = matrix[...]
    bound = jnp.max(jnp.sum(jnp.abs(full), axis=1, keepdims=True), axis=0, keepdims=True)
    unit = 1.0 / bound
    factor = (full * unit).astype(jnp.bfloat16)
    row_ids = lax.broadcasted_iota(jnp.int32, (band, order_size), 0) + r * band
    ones = (row_ids == lax.broadcasted_iota(jnp.int32, (band, order_size), 1)).astype(jnp.float32)
    total = 2.0 * ones - matrix[pl.ds(pl.multiple_of(r * band, 8), band), :] * unit
    for _ in range(TERMS - 2):
        product = jnp.dot(
            total.astype(jnp.bfloat16), factor, preferred_element_type=jnp.float32
        )
        total = ones + total - product
    inv_ref[0] = total * unit

    def drain_ring(some_parts):
        for part in some_parts:
            for way in range(2):
                for hop in range(hops(way, part)):
                    ring_copy(way, hop, part).wait_send()

    drain_ring((0, 1))

    @pl.when(borrows)
    def _():
        for i in range(bands):
            lend(i).wait_send()

    @pl.when(jnp.logical_not(borrows))
    def _():
        drain_ring((2,))

    @pl.when(lends)
    def _():
        for way in range(2):
            for hop in range(lent_hops[way]):
                for i in range(bands):
                    relay_copy(way, hop, i).wait_send()
                    give_back(way, hop, i).wait_send()

    sib_wait.wait_send()
    copy(some_old, some_old, old_sem.at[0], old_sem.at[1], dp=sibling).wait_send()
    pass_old.wait_send()

    def drain(c, _):
        feats_in(c, 0).wait_send()
        if far:
            feats_in(c, 1).wait_send()
        feats_pass(c).wait_send()
        store(out, c, out_ref, store_sem.at[0, c]).wait()
        store(grad, c, grad_ref, store_sem.at[1, c]).wait()

        @pl.when(jnp.logical_not(last))
        def _():
            copy(out.at[c], x_in.at[c], fwd_send.at[c], fwd_recv.at[c], section=up).wait_send()

        @pl.when(jnp.logical_not(first))
        def _():
            copy(grad.at[c], g_in.at[c], bwd_send.at[c], bwd_recv.at[c], section=down).wait_send()

        return 0

    lax.fori_loop(0, micro, drain, 0)


def shards(sections, replicas, inputs, cotangent, weights, old_factor, plan, order):
    micro, rows, width = inputs.shape
    _, blocks, band, order_size = old_factor.shape
    shard = weights.shape[1]
    lent_rows = shard // 16 * 3 // 10 * 16
    pieces = 5 if width % 640 == 0 else width // 128
    vmem = pl.BlockSpec(memory_space=pltpu.VMEM)
    smem = pl.BlockSpec(memory_space=pltpu.SMEM)
    free = pl.BlockSpec(memory_space=pl.ANY)
    hbm = pl.BlockSpec(memory_space=pltpu.HBM)
    sems = pltpu.SemaphoreType.DMA
    zs = replicas // CORES
    acts = pltpu.VMEM((micro, rows, width), jnp.bfloat16)
    return pl.pallas_call(
        functools.partial(kernel, sections, replicas, pieces),
        out_shape=(
            jax.ShapeDtypeStruct((1, micro, rows, width), jnp.bfloat16),
            jax.ShapeDtypeStruct((1, micro, rows, width), jnp.bfloat16),
            jax.ShapeDtypeStruct((1, band, order_size), jnp.float32),
        ),
        in_specs=[smem, smem, hbm, hbm, hbm, hbm],
        out_specs=(free, free, vmem),
        scratch_shapes=[
            pltpu.VMEM((width, width), jnp.bfloat16),
            pltpu.VMEM((width, width), jnp.bfloat16),
            acts,
            acts,
            acts,
            acts,
            acts,
            pltpu.VMEM((micro, rows, width), jnp.float32),
            acts,
            pltpu.VMEM((micro, CORES, zs, rows, order_size), jnp.bfloat16),
            pltpu.VMEM((blocks, band, order_size), jnp.float32),
            pltpu.VMEM((zs, CORES, band, order_size), jnp.float32),
            pltpu.VMEM((order_size, order_size), jnp.float32),
            pltpu.VMEM((zs, lent_rows, width), jnp.bfloat16),
            sems((3,)),
            sems((2, micro)),
            sems((2, 3 * (zs // 2))),
            sems((2, 3 * (zs // 2))),
            sems((2,)),
            sems((2, lent_rows // BAND)),
            sems((2, zs // 2, lent_rows // BAND)),
            sems((2, zs // 2, lent_rows // BAND)),
            sems((2, zs // 2, lent_rows // BAND)),
            sems((2, zs // 2, lent_rows // BAND)),
            sems((micro,)),
            sems((micro,)),
            sems((micro,)),
            sems((micro,)),
            sems((2, micro)),
            sems((2, micro)),
            sems((micro,)),
            sems((micro,)),
            sems((2,)),
            sems((2,)),
        ],
        compiler_params=pltpu.CompilerParams(
            collective_id=0, has_side_effects=True, vmem_limit_bytes=52 * 2**20
        ),
    )(plan.T, order, inputs, cotangent, weights, old_factor)


def solution(mesh):
    return jax.shard_map(
        functools.partial(shards, mesh.shape["section"], mesh.shape["dp"]),
        mesh=mesh,
        in_specs=(
            P(None, "dp", None),
            P(None, "dp", None),
            P("section", "dp", None),
            P("section", None, "dp", None),
            P(),
            P(),
        ),
        out_specs=(
            P("section", None, "dp", None),
            P("section", None, "dp", None),
            P("section", "dp", None),
        ),
        check_vma=False,
    )
```

```python
import functools

import jax
import jax.numpy as jnp
from jax import lax
from jax.experimental import pallas as pl
from jax.experimental.pallas import tpu as pltpu
from jax.sharding import PartitionSpec as P

RETAIN = 0.6
DAMPING = 0.1
TERMS = 8
CORES = 2
BAND = 16
MESH = pl.DeviceIdType.MESH


def kernel(
    sections,
    replicas,
    pieces,
    plan_ref,
    order_ref,
    x_ref,
    ct_ref,
    w_ref,
    old_ref,
    out_ref,
    grad_ref,
    inv_ref,
    w,
    wt,
    ends,
    x_in,
    g_in,
    out,
    grad,
    slope,
    delta,
    feats,
    old_own,
    old_all,
    matrix,
    lent,
    local_sem,
    store_sem,
    ring_send,
    ring_recv,
    sib_sem,
    lend_sem,
    relay_send,
    relay_recv,
    back_send,
    back_recv,
    fwd_send,
    fwd_recv,
    bwd_send,
    bwd_recv,
    feat_send,
    feat_recv,
    feat_pass,
    feat_got,
    old_sem,
    old_pass,
):
    micro, rows, width = x_in.shape
    shard = w_ref.shape[1]
    band, order_size = old_ref.shape[2], old_ref.shape[3]
    piece = width // pieces
    zs = replicas // CORES
    lent_rows = lent.shape[1]
    bands = lent_rows // BAND
    parts = (
        (0, shard - 2 * lent_rows),
        (shard - 2 * lent_rows, lent_rows),
        (shard - lent_rows, lent_rows),
    )
    group = max(1, sections // 4)
    s = lax.axis_index("section")
    r = lax.axis_index("dp")
    z, core = r // CORES, r % CORES
    first, last = s == 0, s == sections - 1
    borrows, lends = s < group, s >= sections - group
    partner = (s + sections - group) % sections
    partner = jnp.where(borrows, partner, jnp.where(lends, s - (sections - group), s))
    sibling = z * CORES + (1 - core)
    up, down = jnp.minimum(s + 1, sections - 1), jnp.maximum(s - 1, 0)

    def along_z(steps):
        return (z + steps) % zs

    def copy(src, dst, send, recv, **device):
        return pltpu.make_async_remote_copy(
            src_ref=src,
            dst_ref=dst,
            send_sem=send,
            recv_sem=recv,
            device_id=device,
            device_id_type=MESH,
        )

    own_w = pltpu.make_async_copy(
        w_ref.at[0], w.at[pl.ds(pl.multiple_of(r * shard, 16), shard)], local_sem.at[0]
    )
    own_w.start()
    load_old = pltpu.make_async_copy(old_ref.at[0], old_own, local_sem.at[1])
    load_old.start()
    load_x = pltpu.make_async_copy(x_ref, ends, local_sem.at[2])
    load_ct = pltpu.make_async_copy(ct_ref, ends, local_sem.at[2])

    @pl.when(first)
    def _():
        load_x.start()

    @pl.when(last)
    def _():
        load_ct.start()

    barrier = pltpu.get_barrier_semaphore()

    def greet(i, _):
        there = along_z(i) * CORES + core
        pl.semaphore_signal(barrier, inc=1, device_id={"dp": there}, device_id_type=MESH)
        return 0

    lax.fori_loop(1, zs, greet, 0)
    pl.semaphore_signal(barrier, inc=1, device_id={"dp": sibling}, device_id_type=MESH)
    helped = jnp.logical_or(borrows, lends)

    @pl.when(jnp.logical_not(last))
    def _():
        pl.semaphore_signal(barrier, inc=1, device_id={"section": up}, device_id_type=MESH)

    @pl.when(jnp.logical_not(first))
    def _():
        pl.semaphore_signal(barrier, inc=1, device_id={"section": down}, device_id_type=MESH)

    @pl.when(helped)
    def _():
        pl.semaphore_signal(barrier, inc=1, device_id={"section": partner}, device_id_type=MESH)

    peers = zs + jnp.where(first, 0, 1) + jnp.where(last, 0, 1) + jnp.where(helped, 1, 0)
    pl.semaphore_wait(barrier, peers)

    def w_rows(at_z, part):
        start = (at_z * CORES + core) * shard + parts[part][0]
        return w.at[pl.ds(pl.multiple_of(start, 16), parts[part][1])]

    def own_rows(part):
        return w_ref.at[0, pl.ds(*parts[part])]

    def to_sibling(rows_there):
        copy(rows_there, rows_there, sib_sem.at[0], sib_sem.at[1], dp=sibling).start()

    def next_z(way):
        return along_z(1 if way == 0 else zs - 1) * CORES + core

    def from_z(way, hop):
        return along_z(zs - hop if way == 0 else hop)

    def hops(way, part):
        return zs // 2 if (way == 0) == (part == 0) else zs // 2 - 1

    def ring_copy(way, hop, part):
        spot = hop * 3 + part
        dst = w_rows(from_z(way, hop), part)
        src = own_rows(part) if hop == 0 else dst
        return copy(src, dst, ring_send.at[way, spot], ring_recv.at[way, spot], dp=next_z(way))

    def ring_arrival(way, hop, part):
        spot = hop * 3 + part
        here = w_rows(from_z(way, hop + 1), part)
        copy(
            here, here, ring_send.at[way, spot], ring_recv.at[way, spot], dp=next_z(way)
        ).wait_recv()
        return here

    def lent_band(at_z, i):
        return lent.at[at_z, pl.ds(i * BAND, BAND)]

    def lend(i):
        start = parts[2][0] + i * BAND
        return copy(
            w_ref.at[0, pl.ds(start, BAND)],
            lent_band(z, i),
            lend_sem.at[0, i],
            lend_sem.at[1, i],
            section=partner,
        )

    def relay_copy(way, hop, i, at=0):
        here = lent_band(from_z(way, hop + at), i)
        return copy(
            here, here, relay_send.at[way, hop, i], relay_recv.at[way, hop, i], dp=next_z(way)
        )

    def give_back(way, hop, i):
        at_z = from_z(way, hop + 1)
        start = (at_z * CORES + core) * shard + parts[2][0] + i * BAND
        return copy(
            lent_band(at_z, i),
            w.at[pl.ds(pl.multiple_of(start, 16), BAND)],
            back_send.at[way, hop, i],
            back_recv.at[way, hop, i],
            section=partner,
        )

    def back_arrival(way, hop):
        for i in range(bands):
            give_back(way, hop, i).wait_recv()
        to_sibling(w_rows(from_z(way, hop + 1), 2))

    lent_hops = (zs // 2, zs // 2 - 1)

    def ring(some_parts, extra):
        for hop in range(zs // 2 + 1):
            for part in some_parts:
                for way in range(2):
                    came = None
                    if 0 < hop <= hops(way, part):
                        came = ring_arrival(way, hop - 1, part)
                    if hop < hops(way, part):
                        ring_copy(way, hop, part).start()
                    if came is not None:
                        to_sibling(came)
            if hop == 0:
                own_w.wait()
                to_sibling(w.at[pl.ds(pl.multiple_of(r * shard, 16), shard)])
            if hop >= 2:
                extra(hop - 2)
        extra(zs // 2 - 1)

    @pl.when(borrows)
    def _():
        for i in range(bands):
            lend(i).start()

        def extra(hop):
            for way in range(2):
                if hop < lent_hops[way]:
                    back_arrival(way, hop)

        ring((0, 1), extra)

    @pl.when(lends)
    def _():
        for hop in range(zs // 2 + 1):
            for i in range(bands):
                if hop == 0:
                    lend(i).wait_recv()
                for way in range(2):
                    came = 0 < hop <= lent_hops[way]
                    if came:
                        relay_copy(way, hop - 1, i, 1).wait_recv()
                    if hop < lent_hops[way]:
                        relay_copy(way, hop, i).start()
                    if came:
                        give_back(way, hop - 1, i).start()

    @pl.when(jnp.logical_not(borrows))
    def _():
        ring((0, 1, 2), lambda hop: None)

    load_old.wait()
    block = plan_ref[0, s]
    filled = plan_ref[2, s]
    old_all[z, core] = old_own[block]

    def send_old(i, _):
        here = old_all.at[z, core]
        copy(here, here, old_sem.at[0], old_sem.at[1], dp=along_z(i) * CORES + core).start()
        return 0

    lax.fori_loop(1, zs, send_old, 0)
    all_sib = w.at[pl.ds(0, zs * shard)]
    sib_wait = copy(all_sib, all_sib, sib_sem.at[0], sib_sem.at[1], dp=sibling)
    sib_wait.wait_recv()

    def turn_weights():
        tile = 2 * 128
        spots = lax.broadcasted_iota(jnp.int32, (tile, tile), 0)
        eye = (spots == lax.broadcasted_iota(jnp.int32, (tile, tile), 1)).astype(jnp.bfloat16)

        def turn(i, _):
            at = pl.ds(pl.multiple_of(i * tile, tile), tile)
            for j in range(pieces):
                cols = pl.ds(j * piece, piece)
                wt[cols, at] = lax.dot_general(
                    w[at, cols], eye, (((0,), (0,)), ((), ())), preferred_element_type=jnp.float32
                ).astype(jnp.bfloat16)
            return 0

        lax.fori_loop(0, width // tile, turn, 0)

    def store(ref, c, whole_ref, sem):
        return pltpu.make_async_copy(ref.at[c], whole_ref.at[0, c], sem)

    def by_pieces(value, matrix_ref, finish):
        before = None
        for j in range(pieces):
            cols = pl.ds(j * piece, piece)
            product = jnp.dot(value, matrix_ref[:, cols], preferred_element_type=jnp.float32)
            if before is not None:
                finish(*before)
            before = (cols, product)
        finish(*before)

    def forward(c, count, sends):
        for i in range(count):
            arrival = copy(
                x_in.at[c + i], x_in.at[c + i], fwd_send.at[c + i], fwd_recv.at[c + i], section=up
            )
            if sends:

                @pl.when(first)
                def _():
                    x_in[c + i] = ends[order_ref[c + i]]

                @pl.when(jnp.logical_not(first))
                def _():
                    arrival.wait_recv()

            else:
                arrival.wait_recv()

        these = pl.ds(c, count)
        x = x_in[these].reshape(count * rows, width)

        def finish(cols, pre):
            pre = pre.reshape(count, rows, piece)
            gate = jax.nn.sigmoid(pre)
            out[these, :, cols] = (x_in[these, :, cols].astype(jnp.float32) + pre * gate).astype(
                jnp.bfloat16
            )
            if sends:
                copy(
                    out.at[c, :, cols],
                    x_in.at[c, :, cols],
                    fwd_send.at[c],
                    fwd_recv.at[c],
                    section=up,
                ).start()
            slope[these, :, cols] = gate * (1.0 + pre * (1.0 - gate))

        by_pieces(x, w, finish)
        for i in range(count):
            store(out, c + i, out_ref, store_sem.at[0, c + i]).start()

    def forward_step(c, _):
        forward(c, 1, True)
        return 0

    @pl.when(first)
    def _():
        load_x.wait()

    @pl.when(s >= sections // 2)
    def _():
        turn_weights()

    @pl.when(jnp.logical_not(last))
    def _():
        lax.fori_loop(0, micro, forward_step, 0)

    @pl.when(s < sections // 2)
    def _():
        turn_weights()

    own_old = old_all.at[:, core]
    some_old = old_all.at[pl.ds(0, zs - 1), core]
    copy(some_old, some_old, old_sem.at[0], old_sem.at[1], dp=sibling).wait_recv()
    pass_old = copy(own_old, own_old, old_pass.at[0], old_pass.at[1], dp=sibling)
    pass_old.start()
    pass_old.wait_recv()
    scale = (1.0 - RETAIN) / (filled * (rows * replicas)).astype(jnp.float32)
    spots = lax.broadcasted_iota(jnp.int32, (order_size, order_size), 0)
    eye = spots == lax.broadcasted_iota(jnp.int32, (order_size, order_size), 1)
    matrix[...] = RETAIN * old_all[...].reshape(order_size, order_size) + jnp.where(
        eye, DAMPING, 0.0
    )
    place = block % (width // order_size)
    from_input = block < width // order_size

    def gradient_in(c):
        @pl.when(last)
        def _():
            g_in[c] = ends[order_ref[c]]

        @pl.when(jnp.logical_not(last))
        def _():
            copy(g_in.at[c], g_in.at[c], bwd_send.at[c], bwd_recv.at[c], section=down).wait_recv()

        delta[c] = (g_in[c].astype(jnp.float32) * slope[c]).astype(jnp.bfloat16)

    def choose_features(c):
        chosen = jnp.zeros((rows, order_size), jnp.bfloat16)
        for j in range(width // order_size):
            cols = pl.ds(j * order_size, order_size)
            here = jnp.where(from_input, x_in[c, :, cols], delta[c, :, cols])
            chosen = jnp.where(place == j, here, chosen)
        feats[c, core, z] = jnp.where(c < filled, chosen, jnp.zeros_like(chosen))


    right, left = range(1, zs // 2 + 1), range(1, (zs - 1) // 2 + 1)
    near = [d for d in right if d <= 2] + [-d for d in left if d <= 2]
    far = [d for d in right if d > 2] + [-d for d in left if d > 2]

    def send_feats(c, origin, steps, which):
        here = feats.at[c, core, along_z(zs + origin)]
        there = along_z(zs + steps) * CORES + core
        copy(here, here, feat_send.at[which, c], feat_recv.at[which, c], dp=there).start()

    def feats_in(c, which):
        some = feats.at[c, core, pl.ds(0, len(far) if which else len(near))]
        return copy(some, some, feat_send.at[which, c], feat_recv.at[which, c], dp=sibling)

    def send_on(c):
        feats_in(c, 0).wait_recv()
        for d in far:
            way = 1 - 2 * core if d == zs // 2 else (1 if d > 0 else -1)
            send_feats(c, -2 * way, (abs(d) - 2) * way, 1)

    def share_features(c):
        choose_features(c)

        @pl.when(c == micro - 1)
        def _():
            for d in sorted(far, key=abs, reverse=True):
                send_feats(c, 0, d, 1)

        for d in sorted(near, key=abs, reverse=True):
            send_feats(c, 0, d, 0)

        @pl.when(c >= 2)
        def _():
            send_on(c - 2)

    def feats_pass(c):
        here = feats.at[c, core]
        return copy(here, here, feat_pass.at[c], feat_got.at[c], dp=sibling)

    def pass_features(c, _=0):
        @pl.when(c == micro - 1)
        def _():
            feats_in(c, 0).wait_recv()

        if far:
            feats_in(c, 1).wait_recv()
        feats_pass(c).start()
        return 0

    def add_stats(c, _=0):
        feats_pass(c).wait_recv()
        v = feats[c].reshape(replicas * rows, order_size)
        matrix[...] += scale * lax.dot_general(
            v, v, (((0,), (0,)), ((), ())), preferred_element_type=jnp.float32
        )
        return 0

    def backward(c, count):
        for i in range(count):
            gradient_in(c + i)
        these = pl.ds(c, count)
        d = delta[these].reshape(count * rows, width)

        def finish(cols, back):
            back = back.reshape(count, rows, piece)
            grad[these, :, cols] = (g_in[these, :, cols].astype(jnp.float32) + back).astype(
                jnp.bfloat16
            )
            copy(
                grad.at[c, :, cols],
                g_in.at[c, :, cols],
                bwd_send.at[c],
                bwd_recv.at[c],
                section=down,
            ).start()

        by_pieces(d, wt, finish)
        for i in range(1, count):
            copy(
                grad.at[c + i], g_in.at[c + i], bwd_send.at[c + i], bwd_recv.at[c + i], section=down
            ).start()
        for i in range(count):
            share_features(c + i)
            store(grad, c + i, grad_ref, store_sem.at[1, c + i]).start()

    def backward_step(c, _):
        backward(c, 1)
        return 0

    near_last = jnp.logical_and(s >= sections - 2, jnp.logical_not(first))

    @pl.when(jnp.logical_not(jnp.logical_or(first, near_last)))
    def _():
        lax.fori_loop(0, micro, backward_step, 0)

    @pl.when(near_last)
    def _():
        @pl.when(last)
        def _():
            load_ct.wait()

        def turn_round(c, count):
            @pl.when(last)
            def _():
                forward(c, count, False)

            backward(c, count)

        def by_twos(i, _):
            turn_round(1 + 2 * i, 2)
            return 0

        turn_round(0, 1)
        lax.fori_loop(0, (micro - 2) // 2, by_twos, 0)
        turn_round(micro - 1, 1)

    @pl.when(jnp.logical_not(first))
    def _():
        send_on(micro - 2)
        lax.fori_loop(0, micro, pass_features, 0)
        lax.fori_loop(0, micro, add_stats, 0)

    lag = min(4, micro - 1)

    def backward_first(c, _):
        gradient_in(c)
        share_features(c)

        @pl.when(c >= lag)
        def _():
            pass_features(c - lag)

        @pl.when(c > lag)
        def _():
            add_stats(c - lag - 1)

        return 0

    @pl.when(first)
    def _():
        lax.fori_loop(0, micro, backward_first, 0)
        send_on(micro - 2)

        def all_gradients(j, _):
            cols = pl.ds(pl.multiple_of(j * piece, 128), piece)
            d = delta[...].reshape(micro * rows, width)
            back = jnp.dot(d, wt[:, cols], preferred_element_type=jnp.float32)
            total = g_in[:, :, cols].astype(jnp.float32) + back.reshape(micro, rows, piece)
            grad[:, :, cols] = total.astype(jnp.bfloat16)
            return 0

        lax.fori_loop(0, pieces, all_gradients, 0)

        def store_all(c, _):
            store(grad, c, grad_ref, store_sem.at[1, c]).start()
            return 0

        lax.fori_loop(0, micro, store_all, 0)
        add_stats(micro - lag - 1)
        lax.fori_loop(micro - lag, micro - 2, pass_features, 0)
        lax.fori_loop(micro - lag, micro - 2, add_stats, 0)
        pass_features(micro - 2)
        pass_features(micro - 1)
        add_stats(micro - 2)
        add_stats(micro - 1)

    full = matrix[...]
    bound = jnp.max(jnp.sum(jnp.abs(full), axis=1, keepdims=True), axis=0, keepdims=True)
    unit = 1.0 / bound
    factor = (full * unit).astype(jnp.bfloat16)
    row_ids = lax.broadcasted_iota(jnp.int32, (band, order_size), 0) + r * band
    ones = (row_ids == lax.broadcasted_iota(jnp.int32, (band, order_size), 1)).astype(jnp.float32)
    total = 2.0 * ones - matrix[pl.ds(pl.multiple_of(r * band, 8), band), :] * unit
    for _ in range(TERMS - 2):
        product = jnp.dot(
            total.astype(jnp.bfloat16), factor, preferred_element_type=jnp.float32
        )
        total = ones + total - product
    inv_ref[0] = total * unit

    def drain_ring(some_parts):
        for part in some_parts:
            for way in range(2):
                for hop in range(hops(way, part)):
                    ring_copy(way, hop, part).wait_send()

    drain_ring((0, 1))

    @pl.when(borrows)
    def _():
        for i in range(bands):
            lend(i).wait_send()

    @pl.when(jnp.logical_not(borrows))
    def _():
        drain_ring((2,))

    @pl.when(lends)
    def _():
        for way in range(2):
            for hop in range(lent_hops[way]):
                for i in range(bands):
                    relay_copy(way, hop, i).wait_send()
                    give_back(way, hop, i).wait_send()

    sib_wait.wait_send()
    copy(some_old, some_old, old_sem.at[0], old_sem.at[1], dp=sibling).wait_send()
    pass_old.wait_send()

    def drain(c, _):
        feats_in(c, 0).wait_send()
        if far:
            feats_in(c, 1).wait_send()
        feats_pass(c).wait_send()
        store(out, c, out_ref, store_sem.at[0, c]).wait()
        store(grad, c, grad_ref, store_sem.at[1, c]).wait()

        @pl.when(jnp.logical_not(last))
        def _():
            copy(out.at[c], x_in.at[c], fwd_send.at[c], fwd_recv.at[c], section=up).wait_send()

        @pl.when(jnp.logical_not(first))
        def _():
            copy(grad.at[c], g_in.at[c], bwd_send.at[c], bwd_recv.at[c], section=down).wait_send()

        return 0

    lax.fori_loop(0, micro, drain, 0)


def shards(sections, replicas, inputs, cotangent, weights, old_factor, plan, order):
    micro, rows, width = inputs.shape
    _, blocks, band, order_size = old_factor.shape
    shard = weights.shape[1]
    lent_rows = shard // 16 * 3 // 10 * 16
    pieces = 5 if width % 640 == 0 else width // 128
    vmem = pl.BlockSpec(memory_space=pltpu.VMEM)
    smem = pl.BlockSpec(memory_space=pltpu.SMEM)
    free = pl.BlockSpec(memory_space=pl.ANY)
    hbm = pl.BlockSpec(memory_space=pltpu.HBM)
    sems = pltpu.SemaphoreType.DMA
    zs = replicas // CORES
    acts = pltpu.VMEM((micro, rows, width), jnp.bfloat16)
    return pl.pallas_call(
        functools.partial(kernel, sections, replicas, pieces),
        out_shape=(
            jax.ShapeDtypeStruct((1, micro, rows, width), jnp.bfloat16),
            jax.ShapeDtypeStruct((1, micro, rows, width), jnp.bfloat16),
            jax.ShapeDtypeStruct((1, band, order_size), jnp.float32),
        ),
        in_specs=[smem, smem, hbm, hbm, hbm, hbm],
        out_specs=(free, free, vmem),
        scratch_shapes=[
            pltpu.VMEM((width, width), jnp.bfloat16),
            pltpu.VMEM((width, width), jnp.bfloat16),
            acts,
            acts,
            acts,
            acts,
            acts,
            pltpu.VMEM((micro, rows, width), jnp.float32),
            acts,
            pltpu.VMEM((micro, CORES, zs, rows, order_size), jnp.bfloat16),
            pltpu.VMEM((blocks, band, order_size), jnp.float32),
            pltpu.VMEM((zs, CORES, band, order_size), jnp.float32),
            pltpu.VMEM((order_size, order_size), jnp.float32),
            pltpu.VMEM((zs, lent_rows, width), jnp.bfloat16),
            sems((3,)),
            sems((2, micro)),
            sems((2, 3 * (zs // 2))),
            sems((2, 3 * (zs // 2))),
            sems((2,)),
            sems((2, lent_rows // BAND)),
            sems((2, zs // 2, lent_rows // BAND)),
            sems((2, zs // 2, lent_rows // BAND)),
            sems((2, zs // 2, lent_rows // BAND)),
            sems((2, zs // 2, lent_rows // BAND)),
            sems((micro,)),
            sems((micro,)),
            sems((micro,)),
            sems((micro,)),
            sems((2, micro)),
            sems((2, micro)),
            sems((micro,)),
            sems((micro,)),
            sems((2,)),
            sems((2,)),
        ],
        compiler_params=pltpu.CompilerParams(
            collective_id=0, has_side_effects=True, vmem_limit_bytes=52 * 2**20
        ),
    )(plan.T, order, inputs, cotangent, weights, old_factor)


def solution(mesh):
    return jax.shard_map(
        functools.partial(shards, mesh.shape["section"], mesh.shape["dp"]),
        mesh=mesh,
        in_specs=(
            P(None, "dp", None),
            P(None, "dp", None),
            P("section", "dp", None),
            P("section", None, "dp", None),
            P(),
            P(),
        ),
        out_specs=(
            P("section", None, "dp", None),
            P("section", None, "dp", None),
            P("section", "dp", None),
        ),
        check_vma=False,
    )
```
